32 devices in a mesh: replica: 8 (over y, x, core), shard: 4 (over z).
Axes of the slice: x: 2, y: 2, z: 4, core: 2. Of those that a mesh axis runs over, the one named last changes fastest.
Arguments:
- layer_input: bfloat16 [4096, 2560], P(('replica', 'shard')), may hold values from -6 to 6
- cotangent: bfloat16 [4096, 2560], P(('replica', 'shard')), may hold values from -6 to 6
- lengths: int32 [8, 3], P('replica'), may hold values from 1 to 510, as said below
- expert_ids: int32 [4096, 1], P(('replica', 'shard')), may hold values from 0 to 1
- g1: bfloat16 [2560], P('shard'), may hold values from 0.5 to 1.5
- wq: bfloat16 [2560, 2560], P('shard'), may hold values from -0.25 to 0.25
- wk: bfloat16 [2560, 512], P('shard'), may hold values from -0.125 to 0.125
- wv: bfloat16 [2560, 512], P('shard'), may hold values from -0.125 to 0.125
- wo: bfloat16 [2560, 2560], P('shard'), may hold values from -0.625 to 0.625
- g2: bfloat16 [2560], P('shard'), may hold values from 0.5 to 1.5
- wr: bfloat16 [2560, 2], P('shard'), may hold values from -0.078125 to 0.078125
- w_su: bfloat16 [2560, 6144], P('shard'), may hold values from -0.125 to 0.125
- w_sd: bfloat16 [3072, 2560], P('shard'), may hold values from -0.109375 to 0.109375
- w_eu: bfloat16 [2560, 2, 3072], P('shard'), may hold values from -0.125 to 0.125
- w_ed: bfloat16 [1536, 2, 2560], P('shard'), may hold values from -0.15625 to 0.15625
Outputs:
- mixed: bfloat16 [4096, 2560], P(('replica', 'shard'))
- input_grad: bfloat16 [4096, 2560], P(('replica', 'shard'))
- g1_grad: float32 [2560], P('shard')
- wq_grad: float32 [2560, 2560], P('shard')
- wk_grad: float32 [2560, 512], P('shard')
- wv_grad: float32 [2560, 512], P('shard')
- wo_grad: float32 [2560, 2560], P('shard')
- g2_grad: float32 [2560], P('shard')
- wr_grad: float32 [2560, 2], P('shard')
- w_su_grad: float32 [2560, 6144], P('shard')
- w_sd_grad: float32 [3072, 2560], P('shard')
- w_eu_grad: float32 [2560, 2, 3072], P('shard')
- w_ed_grad: float32 [1536, 2, 2560], P('shard')
The draws below stay inside these ranges and needn't reach their ends.
Inputs may be any that keep to these rules, and one draw needn't show every extreme that they name: `lengths`: each row sums to 512; one of its documents, at a place drawn from the seed, is at least 448 long. `expert_ids`: each row names one expert.
All inputs are finite; a program needn't handle non-finite values.
Results may differ from the reference program's by a relative error of at most 0.022.
Values may be sent and summed in bfloat16 or wider, within the bound.
A program may use at most 576 MiB of HBM per device.

```python
import jax
import jax.numpy as jnp
from jax import lax

MODEL_WIDTH = 2560
QUERY_HEADS = 20
KEY_HEADS = 4
HEAD_SIZE = 128
FF = 1536
SH = 3072
EXPERTS = 2
TOPK = 1
SEQS = 3
TOK_DEV = 128
GROUP_TOKENS = 512
GROUPS = 8
TOKENS = 4096


def draw_lengths(key, part):
    key = jax.random.fold_in(key, 7)
    first_key, second_key = jax.random.split(key)
    short_docs = jax.random.randint(first_key, (GROUPS, 2), 1, TOK_DEV // 4 + 1, dtype=jnp.int32)
    first_row = (jnp.arange(GROUPS, dtype=jnp.int32) == 0)[:, None]
    short_docs = jnp.where(first_row, jnp.ones_like(short_docs), short_docs)
    long_doc = GROUP_TOKENS - jnp.sum(short_docs, axis=1, keepdims=True)
    joined = jnp.concatenate([long_doc, short_docs], axis=1).astype(jnp.int32)
    orders = jax.vmap(lambda one_key: jax.random.permutation(one_key, SEQS))(jax.random.split(second_key, GROUPS))
    return jnp.take_along_axis(joined, orders.astype(jnp.int32), axis=1)


def level_of(stream_key, extent, cuts, least, high):
    def one(axis_at, blocks):
        draws = jax.random.uniform(jax.random.fold_in(jax.random.fold_in(stream_key, 6), axis_at), (blocks,), jnp.float32, least / len(cuts), high / len(cuts))
        return jnp.repeat(jnp.exp(draws), extent[axis_at] // blocks).reshape((-1,) + (1,) * (len(extent) - axis_at - 1))

    level = one(*cuts[0])
    for cut in cuts[1:]:
        level = level * one(*cut)
    return level


def choose_distinct(key, rows, number_of, top, lift):
    sequence = jax.random.permutation(jax.random.fold_in(key, 1), number_of)
    boost = sequence
    for power in range(3):
        boost = boost * boost // number_of
    boost = boost * lift // number_of
    chance = jax.random.randint(jax.random.fold_in(key, 2), (rows, number_of), 0, 4096) + boost
    sure = jax.random.permutation(jax.random.fold_in(key, 3), rows)[jnp.arange(number_of) % rows]
    chance = jnp.where(jnp.arange(rows)[:, None] == sure[None, :], 1 << 14, chance)
    score = chance * number_of + jnp.arange(number_of)
    return lax.top_k(score.astype(jnp.int32), top)[1].astype(jnp.int32)


def scatter_about(rng, extent, deviation, bound, pieces=(), kind=jnp.bfloat16):
    level = level_of(rng, extent, pieces, -0.22, 0.18) if pieces else 1.0
    drawn = jax.random.normal(rng, extent, jnp.float32) * deviation * level
    return jnp.minimum(jnp.maximum(drawn, -bound), bound).astype(kind)


def setup_inputs(seed: int = 0) -> dict:
    splits = jax.random.split(jax.random.key(seed), 16)
    return {
        "layer_input": scatter_about(splits[0], (TOKENS, MODEL_WIDTH), 1.0, 6.0, ((0, 32),)),
        "cotangent": scatter_about(splits[1], (TOKENS, MODEL_WIDTH), 1.0, 6.0, ((0, 32),)),
        "lengths": draw_lengths(jax.random.fold_in(splits[15], 71), 0),
        "expert_ids": choose_distinct(splits[3], TOKENS, EXPERTS, TOPK, 4096),
        "g1": jnp.clip(1.0 + 0.1 * jax.random.normal(splits[4], (MODEL_WIDTH,), jnp.float32), 0.5, 1.5).astype(jnp.bfloat16),
        "wq": scatter_about(splits[5], (MODEL_WIDTH, QUERY_HEADS * HEAD_SIZE), (MODEL_WIDTH // 4) ** -0.5, 0.25, ((0, 4),)),
        "wk": scatter_about(splits[6], (MODEL_WIDTH, KEY_HEADS * HEAD_SIZE), MODEL_WIDTH ** -0.5, 0.125, ((0, 4),)),
        "wv": scatter_about(splits[7], (MODEL_WIDTH, KEY_HEADS * HEAD_SIZE), MODEL_WIDTH ** -0.5, 0.125, ((0, 4),)),
        "wo": scatter_about(splits[8], (QUERY_HEADS * HEAD_SIZE, MODEL_WIDTH), (QUERY_HEADS * HEAD_SIZE // 32) ** -0.5, 0.625, ((0, 4),)),
        "g2": jnp.clip(1.0 + 0.1 * jax.random.normal(splits[9], (MODEL_WIDTH,), jnp.float32), 0.5, 1.5).astype(jnp.bfloat16),
        "wr": scatter_about(splits[10], (MODEL_WIDTH, EXPERTS), (2 * MODEL_WIDTH) ** -0.5, 0.078125, ((0, 4),)),
        "w_su": scatter_about(splits[11], (MODEL_WIDTH, 2 * SH), MODEL_WIDTH ** -0.5, 0.125, ((0, 4),)),
        "w_sd": scatter_about(splits[12], (SH, MODEL_WIDTH), SH ** -0.5, 0.109375, ((0, 4),)),
        "w_eu": scatter_about(splits[13], (MODEL_WIDTH, EXPERTS, 2 * FF), MODEL_WIDTH ** -0.5, 0.125, ((0, 4),)),
        "w_ed": scatter_about(splits[14], (FF, EXPERTS, MODEL_WIDTH), FF ** -0.5, 0.15625, ((0, 4),)),
    }


epsilon = 1e-05
rope_base = 500000.0
highest = lax.Precision.HIGHEST
far_below = -1e+30

@jax.custom_vjp
def lower_bits(v):
    return lax.optimization_barrier(v.astype(jnp.bfloat16)).astype(jnp.float32)

@jax.custom_vjp
def low_back(v):
    return v

def low_keep(v):
    return (lower_bits(v), None)

def low_pass(kept, grad):
    return (grad,)

def back_keep(v):
    return (v, None)

def back_low(kept, grad):
    return (lower_bits(grad),)
lower_bits.defvjp(low_keep, low_pass)
low_back.defvjp(back_keep, back_low)

def layout(lengths_row):
    doc_ends = jnp.cumsum(lengths_row).astype(jnp.int32)
    doc_starts = doc_ends - lengths_row
    places = jnp.arange(GROUP_TOKENS, dtype=jnp.int32)
    document = lax.optimization_barrier(jnp.sum((places[:, None] >= doc_ends[None, :]).astype(jnp.int32), axis=1))
    chosen = (document[:, None] == jnp.arange(SEQS, dtype=jnp.int32)[None, :]).astype(jnp.int32)
    position = places - lax.optimization_barrier(jnp.sum(chosen * doc_starts[None, :], axis=1))
    return (document, position)

def angles(position):
    inverse = rope_base ** (-(jnp.arange(HEAD_SIZE // 2, dtype=jnp.float32) * 2.0) / HEAD_SIZE)
    phases = position.astype(jnp.float32)[:, None] * inverse[None, :]
    return (jnp.cos(phases), jnp.sin(phases))

def apply_rotation(entries, cosine_table, sine_table):
    half_width = HEAD_SIZE // 2
    first_half = entries[..., :half_width]
    second_half = entries[..., half_width:]
    cos_b = cosine_table[:, None, :]
    sin_b = sine_table[:, None, :]
    return jnp.concatenate([first_half * cos_b - second_half * sin_b, second_half * cos_b + first_half * sin_b], axis=-1)

def rms_norm(inputs, gain_row):
    inverse_rms = lax.rsqrt(lax.optimization_barrier(jnp.mean(inputs * inputs, axis=-1, keepdims=True)) + epsilon)
    return inputs * inverse_rms * gain_row

def silu_product(both, split_at):
    gate_part = both[:, :split_at]
    up_part = both[:, split_at:]
    return gate_part * jax.nn.sigmoid(gate_part) * up_part

def attend_head(query_rows, incoming_keys, value_rows, allowed):
    scores = low_back(jnp.einsum('tqd,sd->qts', query_rows, incoming_keys, precision=highest) * HEAD_SIZE ** (-0.5))
    scores = jnp.where(allowed[None], scores, far_below)
    peak_score = lax.optimization_barrier(jnp.max(scores, axis=-1, keepdims=True))
    weights = jnp.where(allowed[None], jnp.exp(scores - peak_score), 0.0)
    probabilities = weights / lax.optimization_barrier(jnp.sum(weights, axis=-1, keepdims=True))
    return jnp.einsum('qts,sd->tqd', lower_bits(probabilities), value_rows, precision=highest)

def forward(hidden, lengths_row, chosen_ids, g1, wq, wk, wv, wo, g2, wr, w_su, w_sd, w_eu, w_ed):
    document, position = layout(lengths_row)
    places = jnp.arange(GROUP_TOKENS, dtype=jnp.int32)
    allowed = (document[:, None] == document[None, :]) & (places[:, None] >= places[None, :])
    cosine_table, sine_table = angles(position)
    normed = lower_bits(rms_norm(hidden, g1))
    query_rows = low_back(jnp.dot(normed, wq, precision=highest))
    incoming_keys = low_back(jnp.dot(normed, wk, precision=highest))
    value_rows = lower_bits(low_back(jnp.dot(normed, wv, precision=highest)))
    query_rows = lower_bits(apply_rotation(query_rows.reshape(GROUP_TOKENS, QUERY_HEADS, HEAD_SIZE), cosine_table, sine_table)).reshape(GROUP_TOKENS, KEY_HEADS, QUERY_HEADS // KEY_HEADS, HEAD_SIZE)
    incoming_keys = lower_bits(apply_rotation(incoming_keys.reshape(GROUP_TOKENS, KEY_HEADS, HEAD_SIZE), cosine_table, sine_table))
    value_rows = value_rows.reshape(GROUP_TOKENS, KEY_HEADS, HEAD_SIZE)
    per_head = jax.checkpoint(lambda queries_h, keys_h, values_h: attend_head(queries_h, keys_h, values_h, allowed))
    mixture = lax.map(lambda record: per_head(record[0], record[1], record[2]), (query_rows.transpose(1, 0, 2, 3), incoming_keys.transpose(1, 0, 2), value_rows.transpose(1, 0, 2)))
    attended = low_back(lower_bits(mixture.transpose(1, 0, 2, 3).reshape(GROUP_TOKENS, QUERY_HEADS * HEAD_SIZE)))
    middle = hidden + low_back(jnp.dot(attended, wo, precision=highest))
    normed = lower_bits(rms_norm(middle, g2))
    logits = low_back(jnp.dot(normed, wr, precision=highest))
    onehot = (chosen_ids[:, :, None] == jnp.arange(EXPERTS, dtype=jnp.int32)[None, None, :]).astype(jnp.float32)
    chosen_mask = lax.optimization_barrier(jnp.sum(onehot, axis=1))
    routed = chosen_mask * jax.nn.softmax(logits, axis=-1)
    shared = lower_bits(silu_product(low_back(jnp.dot(normed, w_su, precision=highest)), SH))
    summed_out = middle + low_back(jnp.dot(shared, w_sd, precision=highest))
    for expert in range(EXPERTS):
        inner = lower_bits(silu_product(low_back(jnp.dot(normed, w_eu[:, expert], precision=highest)), FF))
        summed_out = summed_out + routed[:, expert:expert + 1] * low_back(jnp.dot(inner, w_ed[:, expert], precision=highest))
    return summed_out

def reference(layer_input, cotangent, lengths, expert_ids, g1, wq, wk, wv, wo, g2, wr, w_su, w_sd, w_eu, w_ed):
    weights = tuple((weight.astype(jnp.float32) for weight in (g1, wq, wk, wv, wo, g2, wr, w_su, w_sd, w_eu, w_ed)))
    blocks = (layer_input.reshape(GROUPS, GROUP_TOKENS, MODEL_WIDTH), cotangent.reshape(GROUPS, GROUP_TOKENS, MODEL_WIDTH), lengths, expert_ids.reshape(GROUPS, GROUP_TOKENS, TOPK))

    def advance(totals, record):
        tokens, upstream, lengths_row, chosen = record
        output, pullback = jax.vjp(lambda hidden, *weights_in: forward(hidden, lengths_row, chosen, *weights_in), tokens.astype(jnp.float32), *weights)
        gradients = pullback(upstream.astype(jnp.float32))
        updated = tuple((first_term + second_term for first_term, second_term in zip(totals, gradients[1:])))
        return (updated, (output.astype(jnp.bfloat16), gradients[0].astype(jnp.bfloat16)))
    initial = tuple((jnp.zeros_like(weight) for weight in weights))
    summed, (outputs, input_grads) = lax.scan(advance, initial, blocks)
    return (outputs.reshape(TOKENS, MODEL_WIDTH), input_grads.reshape(TOKENS, MODEL_WIDTH), summed[0], summed[1], summed[2], summed[3], summed[4], summed[5], summed[6], summed[7], summed[8], summed[9], summed[10])
```

```python
import jax
import jax.numpy as jnp
from jax import lax
from jax.sharding import PartitionSpec as P

QUERY_HEADS = 20
KEY_HEADS = 4
HEAD_SIZE = 128
FF = 1536
SH = 3072
EXPERTS = 2
SEQS = 3


epsilon = 1e-05
rope_base = 500000.0
far_below = -1e30


def shortened(array):

    def short(part):
        return part.astype(jnp.bfloat16) if part.dtype == jnp.float32 else part

    return jax.tree.map(short, array)


def angles(position):
    inverse = rope_base ** (-(jnp.arange(HEAD_SIZE // 2, dtype=jnp.float32) * 2.0) / HEAD_SIZE)
    phases = position.astype(jnp.float32)[:, None] * inverse[None, :]
    return (jnp.cos(phases), jnp.sin(phases))


def apply_rotation(entries, cosine_table, sine_table):
    half_width = HEAD_SIZE // 2
    first_half = entries[..., :half_width]
    second_half = entries[..., half_width:]
    cos_b = cosine_table[:, None, :]
    sin_b = sine_table[:, None, :]
    return jnp.concatenate(
        [first_half * cos_b - second_half * sin_b, second_half * cos_b + first_half * sin_b],
        axis=-1,
    )


def reverse_rotation(grads_in, cosine_table, sine_table):
    half_width = HEAD_SIZE // 2
    first_half = grads_in[..., :half_width]
    second_half = grads_in[..., half_width:]
    cos_b = cosine_table[:, None, :]
    sin_b = sine_table[:, None, :]
    return jnp.concatenate(
        [first_half * cos_b + second_half * sin_b, second_half * cos_b - first_half * sin_b],
        axis=-1,
    )


def layout(lengths_row, device_group):
    doc_ends = jnp.cumsum(lengths_row)
    doc_starts = doc_ends - lengths_row
    places = jnp.arange(device_group, dtype=jnp.int32)
    document = jnp.sum((places[:, None] >= doc_ends[None, :]).astype(jnp.int32), axis=1)
    chosen = (document[:, None] == jnp.arange(SEQS, dtype=jnp.int32)[None, :]).astype(jnp.int32)
    position = places - jnp.sum(chosen * doc_starts[None, :], axis=1)
    return (document, position)


def norm_forward(inputs):
    inverse_rms = lax.rsqrt(jnp.mean(inputs * inputs, axis=-1, keepdims=True) + epsilon)
    return (inputs * inverse_rms, inverse_rms)


def norm_backward(grad_out, unit, inverse_rms, gain_row):
    scaled = grad_out * gain_row.astype(jnp.float32)
    grad_in = inverse_rms * (scaled - unit * jnp.mean(scaled * unit, axis=-1, keepdims=True))
    return (grad_in, jnp.sum(grad_out * unit, axis=0))


def silu_product(both, split_at):
    gate_part = both[:, :split_at]
    up_part = both[:, split_at:]
    return gate_part * jax.nn.sigmoid(gate_part) * up_part


def swiglu_back(both, grad_inner, split_at):
    gate_part = both[:, :split_at]
    up_part = both[:, split_at:]
    sigma = jax.nn.sigmoid(gate_part)
    activated = gate_part * sigma
    grad_gate = grad_inner * up_part * sigma * (1.0 + gate_part * (1.0 - sigma))
    return jnp.concatenate([grad_gate, grad_inner * activated], axis=-1)


def matrix_product(left, right):
    return jnp.dot(left, right, preferred_element_type=jnp.float32)


def times_transposed(left, right):
    return jnp.einsum("tf,df->td", left, right, preferred_element_type=jnp.float32)


def weight_grad(left, right):
    return jnp.einsum("td,tf->df", left, right, preferred_element_type=jnp.float32)


def shards(
    layer_input, cotangent, lengths, expert_ids, g1, wq, wk, wv, wo, g2, wr, w_su, w_sd, w_eu, w_ed
):
    token_count = layer_input.shape[0]
    device_group = token_count * lax.axis_size("shard")
    offset = lax.axis_index("shard") * token_count
    group_layout = QUERY_HEADS // KEY_HEADS
    score_scale = HEAD_SIZE ** (-0.5)

    def fetch_attention():
        return (
            lax.all_gather(g1, "shard", axis=0, tiled=True),
            lax.all_gather(wq, "shard", axis=0, tiled=True),
            lax.all_gather(wk, "shard", axis=0, tiled=True),
            lax.all_gather(wv, "shard", axis=0, tiled=True),
            lax.all_gather(wo, "shard", axis=0, tiled=True),
        )

    def reduce_grads(pieces):
        shares = jax.tree.map(
            lambda part: part.astype(jnp.float32),
            lax.psum_scatter(shortened(pieces), "shard", scatter_dimension=0, tiled=True),
        )
        return jax.tree.map(
            lambda part: part.astype(jnp.float32), lax.psum(shortened(shares), "replica")
        )

    document, position = layout(lengths[0], device_group)
    places = jnp.arange(device_group, dtype=jnp.int32)
    query_doc = lax.dynamic_slice_in_dim(document, offset, token_count)
    query_place = offset + jnp.arange(token_count, dtype=jnp.int32)
    allowed = (query_doc[:, None] == document[None, :]) & (query_place[:, None] >= places[None, :])
    cosine_table, sine_table = angles(lax.dynamic_slice_in_dim(position, offset, token_count))
    hidden = layer_input.astype(jnp.float32)
    gain_one, w_query, key_matrix, w_value, w_out = fetch_attention()
    unit_one, rms_one = norm_forward(hidden)
    first_normed = (unit_one * gain_one.astype(jnp.float32)).astype(jnp.bfloat16)
    query_rows = apply_rotation(
        matrix_product(first_normed, w_query).reshape(token_count, QUERY_HEADS, HEAD_SIZE),
        cosine_table,
        sine_table,
    )
    query_rows = query_rows.astype(jnp.bfloat16).reshape(
        token_count, KEY_HEADS, group_layout, HEAD_SIZE
    )
    local_keys = apply_rotation(
        matrix_product(first_normed, key_matrix).reshape(token_count, KEY_HEADS, HEAD_SIZE),
        cosine_table,
        sine_table,
    )
    local_keys = local_keys.astype(jnp.bfloat16).reshape(token_count, KEY_HEADS * HEAD_SIZE)
    values_own = matrix_product(first_normed, w_value).astype(jnp.bfloat16)
    gathered_keys, gathered_values = (
        lax.all_gather(local_keys, "shard", axis=0, tiled=True),
        lax.all_gather(values_own, "shard", axis=0, tiled=True),
    )
    gathered_keys = gathered_keys.reshape(device_group, KEY_HEADS, HEAD_SIZE)
    gathered_values = gathered_values.reshape(device_group, KEY_HEADS, HEAD_SIZE)

    def scores_of(key_value_head):
        raw = jnp.einsum(
            "tqd,sd->qts",
            query_rows[:, key_value_head],
            gathered_keys[:, key_value_head],
            preferred_element_type=jnp.float32,
        )
        return raw * score_scale

    head_outputs = []
    log_totals = []
    for key_value_head in range(KEY_HEADS):
        masked = jnp.where(allowed[None], scores_of(key_value_head), far_below)
        peak_score = jnp.max(masked, axis=-1, keepdims=True)
        weights = jnp.where(allowed[None], jnp.exp(masked - peak_score), 0.0)
        totals = jnp.sum(weights, axis=-1, keepdims=True)
        probabilities = weights / totals
        log_totals.append(peak_score + jnp.log(totals))
        head_outputs.append(
            jnp.einsum(
                "qts,sd->tqd",
                probabilities.astype(jnp.bfloat16),
                gathered_values[:, key_value_head],
                preferred_element_type=jnp.float32,
            )
        )
    attended = (
        jnp.stack(head_outputs, axis=1)
        .reshape(token_count, QUERY_HEADS * HEAD_SIZE)
        .astype(jnp.bfloat16)
    )
    middle = hidden + matrix_product(attended, w_out)
    gain_two, w_router, w_shared_up, w_shared_down, w_experts_up, w_experts_down = (
        lax.all_gather(g2, "shard", axis=0, tiled=True),
        lax.all_gather(wr, "shard", axis=0, tiled=True),
        lax.all_gather(w_su, "shard", axis=0, tiled=True),
        lax.all_gather(w_sd, "shard", axis=0, tiled=True),
        lax.all_gather(w_eu, "shard", axis=0, tiled=True),
        lax.all_gather(w_ed, "shard", axis=0, tiled=True),
    )
    unit_two, rms_two = norm_forward(middle)
    normed_two = (unit_two * gain_two.astype(jnp.float32)).astype(jnp.bfloat16)
    logits = matrix_product(normed_two, w_router)
    onehot = (expert_ids[:, :, None] == jnp.arange(EXPERTS, dtype=jnp.int32)[None, None, :]).astype(
        jnp.float32
    )
    chosen_mask = jnp.sum(onehot, axis=1)
    probs = jax.nn.softmax(logits, axis=-1)
    routed = chosen_mask * probs
    shared_both = matrix_product(normed_two, w_shared_up)
    shared_inner = silu_product(shared_both, SH).astype(jnp.bfloat16)
    summed_out = middle + matrix_product(shared_inner, w_shared_down)
    expert_boths = []
    expert_inners = []
    expert_results = []
    for expert in range(EXPERTS):
        both = matrix_product(normed_two, w_experts_up[:, expert])
        inner = silu_product(both, FF).astype(jnp.bfloat16)
        result = matrix_product(inner, w_experts_down[:, expert])
        summed_out = summed_out + routed[:, expert : expert + 1] * result
        expert_boths.append(both)
        expert_inners.append(inner)
        expert_results.append(result)
    mixed = summed_out.astype(jnp.bfloat16)
    upstream = cotangent.astype(jnp.float32)
    grad_shared_out = upstream.astype(jnp.bfloat16)
    grad_shared_inner = times_transposed(grad_shared_out, w_shared_down)
    grad_shared_both = swiglu_back(shared_both, grad_shared_inner, SH).astype(jnp.bfloat16)
    grad_normed = times_transposed(grad_shared_both, w_shared_up)
    shared_grads = reduce_grads(
        (weight_grad(normed_two, grad_shared_both), weight_grad(shared_inner, grad_shared_out))
    )
    up_grads = []
    down_grads = []
    routed_grads = []
    for expert in range(EXPERTS):
        grad_result = (routed[:, expert : expert + 1] * upstream).astype(jnp.bfloat16)
        routed_grads.append(jnp.sum(upstream * expert_results[expert], axis=-1))
        down_grads.append(weight_grad(expert_inners[expert], grad_result))
        grad_inner = times_transposed(grad_result, w_experts_down[:, expert])
        grad_both = swiglu_back(expert_boths[expert], grad_inner, FF).astype(jnp.bfloat16)
        up_grads.append(weight_grad(normed_two, grad_both))
        grad_normed = grad_normed + times_transposed(grad_both, w_experts_up[:, expert])
    grad_probs = chosen_mask * jnp.stack(routed_grads, axis=1)
    grad_logits = probs * (grad_probs - jnp.sum(probs * grad_probs, axis=-1, keepdims=True))
    grad_logits = grad_logits.astype(jnp.bfloat16)
    grad_router = weight_grad(normed_two, grad_logits)
    grad_normed = grad_normed + times_transposed(grad_logits, w_router)
    grad_middle_norm, grad_gain_two = norm_backward(grad_normed, unit_two, rms_two, gain_two)
    grad_middle = upstream + grad_middle_norm
    expert_grads = reduce_grads(
        (grad_gain_two, grad_router, jnp.stack(up_grads, axis=1), jnp.stack(down_grads, axis=1))
    )
    gain_one, w_query, key_matrix, w_value, w_out = fetch_attention()
    grad_proj_out = grad_middle.astype(jnp.bfloat16)
    grad_out_weight = weight_grad(attended, grad_proj_out)
    grad_attended = (
        times_transposed(grad_proj_out, w_out)
        .astype(jnp.bfloat16)
        .reshape(token_count, KEY_HEADS, group_layout, HEAD_SIZE)
    )
    query_grads = []
    key_gradients = []
    value_gradients = []
    for key_value_head in range(KEY_HEADS):
        scores = scores_of(key_value_head)
        probabilities = jnp.where(allowed[None], jnp.exp(scores - log_totals[key_value_head]), 0.0)
        grad_here = grad_attended[:, key_value_head]
        grad_weights = jnp.einsum(
            "tqd,sd->qts",
            grad_here,
            gathered_values[:, key_value_head],
            preferred_element_type=jnp.float32,
        )
        grad_scores = probabilities * (
            grad_weights - jnp.sum(probabilities * grad_weights, axis=-1, keepdims=True)
        )
        grad_scores = grad_scores.astype(jnp.bfloat16)
        query_grads.append(
            jnp.einsum(
                "qts,sd->tqd",
                grad_scores,
                gathered_keys[:, key_value_head],
                preferred_element_type=jnp.float32,
            )
            * score_scale
        )
        key_gradients.append(
            jnp.einsum(
                "qts,tqd->sd",
                grad_scores,
                query_rows[:, key_value_head],
                preferred_element_type=jnp.float32,
            )
            * score_scale
        )
        value_gradients.append(
            jnp.einsum(
                "qts,tqd->sd",
                probabilities.astype(jnp.bfloat16),
                grad_here,
                preferred_element_type=jnp.float32,
            )
        )
    reduced_keys, values_summed = (
        lax.psum_scatter(
            jnp.stack(key_gradients, axis=1)
            .reshape(device_group, KEY_HEADS * HEAD_SIZE)
            .astype(jnp.bfloat16),
            "shard",
            scatter_dimension=0,
            tiled=True,
        ).astype(jnp.float32),
        lax.psum_scatter(
            jnp.stack(value_gradients, axis=1)
            .reshape(device_group, KEY_HEADS * HEAD_SIZE)
            .astype(jnp.bfloat16),
            "shard",
            scatter_dimension=0,
            tiled=True,
        ).astype(jnp.float32),
    )
    grad_query = reverse_rotation(
        jnp.stack(query_grads, axis=1).reshape(token_count, QUERY_HEADS, HEAD_SIZE),
        cosine_table,
        sine_table,
    )
    grad_query = grad_query.reshape(token_count, QUERY_HEADS * HEAD_SIZE).astype(jnp.bfloat16)
    key_gradient = reverse_rotation(
        reduced_keys.reshape(token_count, KEY_HEADS, HEAD_SIZE), cosine_table, sine_table
    )
    key_gradient = key_gradient.reshape(token_count, KEY_HEADS * HEAD_SIZE).astype(jnp.bfloat16)
    grad_value = values_summed.astype(jnp.bfloat16)
    grad_normed_one = times_transposed(grad_query, w_query) + times_transposed(
        key_gradient, key_matrix
    )
    grad_normed_one = grad_normed_one + times_transposed(grad_value, w_value)
    grad_hidden_norm, grad_gain_one = norm_backward(grad_normed_one, unit_one, rms_one, gain_one)
    grad_of_input = (grad_middle + grad_hidden_norm).astype(jnp.bfloat16)
    attention_grads = reduce_grads(
        (
            grad_gain_one,
            weight_grad(first_normed, grad_query),
            weight_grad(first_normed, key_gradient),
            weight_grad(first_normed, grad_value),
            grad_out_weight,
        )
    )
    return (
        mixed,
        grad_of_input,
        attention_grads[0],
        attention_grads[1],
        attention_grads[2],
        attention_grads[3],
        attention_grads[4],
        expert_grads[0],
        expert_grads[1],
        shared_grads[0],
        shared_grads[1],
        expert_grads[2],
        expert_grads[3],
    )


def gather_columns(parts, piece):
    rank = lax.axis_index("replica")
    mine = [lax.dynamic_slice_in_dim(part, rank * piece, piece, axis=0) for part in parts]
    mine = jnp.concatenate(mine, axis=-1).transpose(1, 0, 2)
    owned = lax.all_to_all(mine, "shard", split_axis=0, concat_axis=0)
    whole = lax.all_gather(owned, "replica", axis=0)
    return whole.reshape(-1, whole.shape[-1])


def scatter_columns(grad, piece):
    share = lax.psum_scatter(grad, "replica", scatter_dimension=0, tiled=True)
    share = share.reshape(-1, piece, grad.shape[-1])
    swapped = lax.all_to_all(share, "shard", split_axis=0, concat_axis=0)
    return lax.all_gather(swapped, "replica", axis=0)


def planes(
    layer_input, cotangent, lengths, expert_ids, g1, wq, wk, wv, wo, g2, wr, w_su, w_sd, w_eu, w_ed
):
    tokens, width = layer_input.shape
    count = lax.axis_size("shard")
    copies = lax.axis_size("replica")
    rows = wq.shape[0]
    piece = rows // copies
    group = tokens * count
    heads = QUERY_HEADS // count
    sh, ff = SH // count, FF // count
    scale = HEAD_SIZE ** (-0.5)
    f32, bf16 = jnp.float32, jnp.bfloat16

    def mixed_order(x):
        return x.reshape(tokens, count, copies, piece).transpose(0, 2, 1, 3).reshape(tokens, width)

    def plain_order(x):
        return x.reshape(tokens, copies, count, piece).transpose(0, 2, 1, 3).reshape(tokens, width)

    def all_tokens(x):
        return lax.all_gather(x, "shard", axis=0, tiled=True)

    def own_tokens(x):
        return lax.psum_scatter(x.astype(bf16), "shard", scatter_dimension=0, tiled=True).astype(f32)

    small = jnp.concatenate([g1[:, None], g2[:, None], wr], axis=1)
    small = lax.all_gather(small, "shard", axis=0, tiled=True)
    gain_one, gain_two, w_router = small[:, 0], small[:, 1], small[:, 2:]
    w_qkv = gather_columns(
        [
            wq.reshape(rows, count, -1),
            wk.reshape(rows, count, -1),
            wv.reshape(rows, count, -1),
        ],
        piece,
    )
    w_up = gather_columns(
        [
            w_su.reshape(rows, 2, count, sh).transpose(0, 2, 1, 3).reshape(rows, count, 2 * sh),
            w_eu.reshape(rows, 2 * EXPERTS, count, ff)
            .transpose(0, 2, 1, 3)
            .reshape(rows, count, 2 * EXPERTS * ff),
        ],
        piece,
    )
    w_down = jnp.concatenate([w_sd, w_ed[:, 0], w_ed[:, 1]], axis=0)
    ids = all_tokens(expert_ids)
    upstream = all_tokens(cotangent)

    document, position = layout(lengths[0], group)
    places = jnp.arange(group, dtype=jnp.int32)
    allowed = (document[:, None] == document[None, :]) & (places[:, None] >= places[None, :])
    cosine_table, sine_table = angles(position)

    hidden = layer_input.astype(f32)
    unit_one, rms_one = norm_forward(hidden)
    n1 = all_tokens(mixed_order((unit_one * gain_one.astype(f32)).astype(bf16)))
    qkv = matrix_product(n1, w_qkv)
    q_width = heads * HEAD_SIZE
    q = apply_rotation(qkv[:, :q_width].reshape(group, heads, HEAD_SIZE), cosine_table, sine_table)
    q = q.astype(bf16)
    k = apply_rotation(
        qkv[:, q_width : q_width + HEAD_SIZE].reshape(group, 1, HEAD_SIZE), cosine_table, sine_table
    )
    k = k.astype(bf16)[:, 0]
    v = qkv[:, q_width + HEAD_SIZE :].astype(bf16)
    scores = jnp.einsum("tqd,sd->qts", q, k, preferred_element_type=f32) * scale
    scores = jnp.where(allowed[None], scores, far_below)
    peak = jnp.max(scores, axis=-1, keepdims=True)
    weights = jnp.where(allowed[None], jnp.exp(scores - peak), 0.0)
    probs_att = weights / jnp.sum(weights, axis=-1, keepdims=True)
    probs_low = probs_att.astype(bf16)
    attended = jnp.einsum("qts,sd->tqd", probs_low, v, preferred_element_type=f32)
    attended = attended.reshape(group, q_width).astype(bf16)
    middle = hidden + own_tokens(matrix_product(attended, wo))
    unit_two, rms_two = norm_forward(middle)
    n2 = all_tokens(mixed_order((unit_two * gain_two.astype(f32)).astype(bf16)))

    router_mixed = w_router.reshape(count, copies, piece, EXPERTS).transpose(1, 0, 2, 3)
    router_mixed = router_mixed.reshape(width, EXPERTS)
    logits = matrix_product(n2, router_mixed)
    chosen = jnp.sum(
        (ids[:, :, None] == jnp.arange(EXPERTS, dtype=jnp.int32)[None, None, :]).astype(f32), axis=1
    )
    probs = jax.nn.softmax(logits, axis=-1)
    routed = chosen * probs
    z = matrix_product(n2, w_up)
    factor = jnp.concatenate(
        [jnp.ones((group, sh), f32)]
        + [jnp.broadcast_to(routed[:, e : e + 1], (group, ff)) for e in range(EXPERTS)],
        axis=1,
    )
    gate = jnp.concatenate(
        [z[:, :sh]] + [z[:, 2 * sh + 2 * e * ff :][:, :ff] for e in range(EXPERTS)], axis=1
    )
    up = jnp.concatenate(
        [z[:, sh : 2 * sh]] + [z[:, 2 * sh + (2 * e + 1) * ff :][:, :ff] for e in range(EXPERTS)],
        axis=1,
    )
    sigma = jax.nn.sigmoid(gate)
    inner = gate * sigma * up
    inner_low = (factor * inner).astype(bf16)
    mixed = (middle + own_tokens(matrix_product(inner_low, w_down))).astype(bf16)
    grad_inner = times_transposed(upstream, w_down)
    grad_down = weight_grad(inner_low, upstream).astype(bf16)
    kept = inner * grad_inner
    routed_grads = jnp.stack(
        [jnp.sum(kept[:, sh + e * ff : sh + (e + 1) * ff], axis=-1) for e in range(EXPERTS)], axis=1
    )
    scaled = factor * grad_inner
    grad_gate = (scaled * up * sigma * (1.0 + gate * (1.0 - sigma))).astype(bf16)
    grad_up = (scaled * gate * sigma).astype(bf16)
    pieces = [grad_gate[:, :sh], grad_up[:, :sh]]
    for e in range(EXPERTS):
        span = slice(sh + e * ff, sh + (e + 1) * ff)
        pieces += [grad_gate[:, span], grad_up[:, span]]
    grad_z = jnp.concatenate(pieces, axis=1)
    grad_probs = chosen * routed_grads
    grad_logits = probs * (grad_probs - jnp.sum(probs * grad_probs, axis=-1, keepdims=True))
    grad_logits = grad_logits.astype(bf16)
    grad_n2 = times_transposed(grad_z, w_up) + times_transposed(grad_logits, router_mixed)
    grad_w_up = weight_grad(n2, grad_z).astype(bf16)
    grad_router = weight_grad(n2, grad_logits)
    grad_router = grad_router.reshape(copies, count, piece, EXPERTS).transpose(1, 0, 2, 3)
    grad_router = grad_router.reshape(width, EXPERTS)

    up_grads = scatter_columns(grad_w_up, piece).astype(f32)
    down_grads = lax.psum(grad_down, "replica").astype(f32)

    grad_n2 = plain_order(own_tokens(grad_n2))
    grad_middle_norm, grad_gain_two = norm_backward(grad_n2, unit_two, rms_two, gain_two)
    grad_middle = cotangent.astype(f32) + grad_middle_norm
    grad_proj = all_tokens(grad_middle.astype(bf16))
    grad_wo = weight_grad(attended, grad_proj).astype(bf16)
    grad_att = times_transposed(grad_proj, wo).astype(bf16).reshape(group, heads, HEAD_SIZE)
    grad_weights = jnp.einsum("tqd,sd->qts", grad_att, v, preferred_element_type=f32)
    grad_scores = probs_att * (
        grad_weights - jnp.sum(probs_att * grad_weights, axis=-1, keepdims=True)
    )
    grad_scores = grad_scores.astype(bf16)
    grad_q = jnp.einsum("qts,sd->tqd", grad_scores, k, preferred_element_type=f32) * scale
    grad_k = jnp.einsum("qts,tqd->sd", grad_scores, q, preferred_element_type=f32) * scale
    grad_v = jnp.einsum("qts,tqd->sd", probs_low, grad_att, preferred_element_type=f32)
    grad_q = reverse_rotation(grad_q, cosine_table, sine_table).reshape(group, q_width)
    grad_k = reverse_rotation(grad_k[:, None], cosine_table, sine_table)[:, 0]
    grad_qkv = jnp.concatenate([grad_q, grad_k, grad_v], axis=1).astype(bf16)
    grad_n1 = times_transposed(grad_qkv, w_qkv)
    grad_w_qkv = weight_grad(n1, grad_qkv).astype(bf16)
    qkv_grads = scatter_columns(grad_w_qkv, piece).astype(f32)
    wo_grad = lax.psum(grad_wo, "replica").astype(f32)
    grad_n1 = plain_order(own_tokens(grad_n1))
    grad_hidden, grad_gain_one = norm_backward(grad_n1, unit_one, rms_one, gain_one)
    input_grad = (grad_middle + grad_hidden).astype(bf16)

    tiny = jnp.concatenate([grad_gain_one[:, None], grad_gain_two[:, None], grad_router], axis=1)
    tiny = lax.psum(tiny, ("replica", "shard"))
    tiny = lax.dynamic_slice_in_dim(tiny, lax.axis_index("shard") * rows, rows, axis=0)

    def rows_of(block, parts):
        block = block.reshape(copies, count, piece, parts, -1)
        return block.transpose(0, 2, 3, 1, 4).reshape(rows, -1)

    return (
        mixed,
        input_grad,
        tiny[:, 0],
        rows_of(qkv_grads[..., :q_width], 1),
        rows_of(qkv_grads[..., q_width : q_width + HEAD_SIZE], 1),
        rows_of(qkv_grads[..., q_width + HEAD_SIZE :], 1),
        wo_grad,
        tiny[:, 1],
        tiny[:, 2:],
        rows_of(up_grads[..., : 2 * sh], 2),
        down_grads[:sh],
        rows_of(up_grads[..., 2 * sh :], 2 * EXPERTS).reshape(rows, EXPERTS, 2 * FF),
        jnp.stack([down_grads[sh + e * ff : sh + (e + 1) * ff] for e in range(EXPERTS)], axis=1),
    )


def solution(mesh):
    return jax.shard_map(
        planes if mesh.shape["shard"] == KEY_HEADS else shards,
        mesh=mesh,
        in_specs=(
            P(("replica", "shard"), None),
            P(("replica", "shard"), None),
            P("replica", None),
            P(("replica", "shard"), None),
            P("shard"),
            P("shard", None),
            P("shard", None),
            P("shard", None),
            P("shard", None),
            P("shard"),
            P("shard", None),
            P("shard", None),
            P("shard", None),
            P("shard", None, None),
            P("shard", None, None),
        ),
        out_specs=(
            P(("replica", "shard"), None),
            P(("replica", "shard"), None),
            P("shard"),
            P("shard", None),
            P("shard", None),
            P("shard", None),
            P("shard", None),
            P("shard"),
            P("shard", None),
            P("shard", None),
            P("shard", None),
            P("shard", None, None),
            P("shard", None, None),
        ),
        check_vma=False,
    )
```

```python
import functools

import jax
import jax.numpy as jnp
from jax import lax
from jax.experimental import pallas as pl
from jax.experimental.pallas import tpu as pltpu
from jax.sharding import PartitionSpec as P

QUERY_HEADS = 20
KEY_HEADS = 4
HEAD_SIZE = 128
FF = 1536
SH = 3072
EXPERTS = 2
SEQS = 3


epsilon = 1e-05
rope_base = 500000.0
far_below = -1e30


def shortened(array):

    def short(part):
        return part.astype(jnp.bfloat16) if part.dtype == jnp.float32 else part

    return jax.tree.map(short, array)


def angles(position):
    inverse = rope_base ** (-(jnp.arange(HEAD_SIZE // 2, dtype=jnp.float32) * 2.0) / HEAD_SIZE)
    phases = position.astype(jnp.float32)[:, None] * inverse[None, :]
    return (jnp.cos(phases), jnp.sin(phases))


def apply_rotation(entries, cosine_table, sine_table):
    half_width = HEAD_SIZE // 2
    first_half = entries[..., :half_width]
    second_half = entries[..., half_width:]
    cos_b = cosine_table[:, None, :]
    sin_b = sine_table[:, None, :]
    return jnp.concatenate(
        [first_half * cos_b - second_half * sin_b, second_half * cos_b + first_half * sin_b],
        axis=-1,
    )


def reverse_rotation(grads_in, cosine_table, sine_table):
    half_width = HEAD_SIZE // 2
    first_half = grads_in[..., :half_width]
    second_half = grads_in[..., half_width:]
    cos_b = cosine_table[:, None, :]
    sin_b = sine_table[:, None, :]
    return jnp.concatenate(
        [first_half * cos_b + second_half * sin_b, second_half * cos_b - first_half * sin_b],
        axis=-1,
    )


def layout(lengths_row, device_group):
    doc_ends = jnp.cumsum(lengths_row)
    doc_starts = doc_ends - lengths_row
    places = jnp.arange(device_group, dtype=jnp.int32)
    document = jnp.sum((places[:, None] >= doc_ends[None, :]).astype(jnp.int32), axis=1)
    chosen = (document[:, None] == jnp.arange(SEQS, dtype=jnp.int32)[None, :]).astype(jnp.int32)
    position = places - jnp.sum(chosen * doc_starts[None, :], axis=1)
    return (document, position)


def norm_forward(inputs):
    inverse_rms = lax.rsqrt(jnp.mean(inputs * inputs, axis=-1, keepdims=True) + epsilon)
    return (inputs * inverse_rms, inverse_rms)


def norm_backward(grad_out, unit, inverse_rms, gain_row):
    scaled = grad_out * gain_row.astype(jnp.float32)
    grad_in = inverse_rms * (scaled - unit * jnp.mean(scaled * unit, axis=-1, keepdims=True))
    return (grad_in, jnp.sum(grad_out * unit, axis=0))


def silu_product(both, split_at):
    gate_part = both[:, :split_at]
    up_part = both[:, split_at:]
    return gate_part * jax.nn.sigmoid(gate_part) * up_part


def swiglu_back(both, grad_inner, split_at):
    gate_part = both[:, :split_at]
    up_part = both[:, split_at:]
    sigma = jax.nn.sigmoid(gate_part)
    activated = gate_part * sigma
    grad_gate = grad_inner * up_part * sigma * (1.0 + gate_part * (1.0 - sigma))
    return jnp.concatenate([grad_gate, grad_inner * activated], axis=-1)


def matrix_product(left, right):
    return jnp.dot(left, right, preferred_element_type=jnp.float32)


def times_transposed(left, right):
    return jnp.einsum("tf,df->td", left, right, preferred_element_type=jnp.float32)


def weight_grad(left, right):
    return jnp.einsum("td,tf->df", left, right, preferred_element_type=jnp.float32)


def shards(
    layer_input, cotangent, lengths, expert_ids, g1, wq, wk, wv, wo, g2, wr, w_su, w_sd, w_eu, w_ed
):
    token_count = layer_input.shape[0]
    device_group = token_count * lax.axis_size("shard")
    offset = lax.axis_index("shard") * token_count
    group_layout = QUERY_HEADS // KEY_HEADS
    score_scale = HEAD_SIZE ** (-0.5)

    def fetch_attention():
        return (
            lax.all_gather(g1, "shard", axis=0, tiled=True),
            lax.all_gather(wq, "shard", axis=0, tiled=True),
            lax.all_gather(wk, "shard", axis=0, tiled=True),
            lax.all_gather(wv, "shard", axis=0, tiled=True),
            lax.all_gather(wo, "shard", axis=0, tiled=True),
        )

    def reduce_grads(pieces):
        shares = jax.tree.map(
            lambda part: part.astype(jnp.float32),
            lax.psum_scatter(shortened(pieces), "shard", scatter_dimension=0, tiled=True),
        )
        return jax.tree.map(
            lambda part: part.astype(jnp.float32), lax.psum(shortened(shares), "replica")
        )

    document, position = layout(lengths[0], device_group)
    places = jnp.arange(device_group, dtype=jnp.int32)
    query_doc = lax.dynamic_slice_in_dim(document, offset, token_count)
    query_place = offset + jnp.arange(token_count, dtype=jnp.int32)
    allowed = (query_doc[:, None] == document[None, :]) & (query_place[:, None] >= places[None, :])
    cosine_table, sine_table = angles(lax.dynamic_slice_in_dim(position, offset, token_count))
    hidden = layer_input.astype(jnp.float32)
    gain_one, w_query, key_matrix, w_value, w_out = fetch_attention()
    unit_one, rms_one = norm_forward(hidden)
    first_normed = (unit_one * gain_one.astype(jnp.float32)).astype(jnp.bfloat16)
    query_rows = apply_rotation(
        matrix_product(first_normed, w_query).reshape(token_count, QUERY_HEADS, HEAD_SIZE),
        cosine_table,
        sine_table,
    )
    query_rows = query_rows.astype(jnp.bfloat16).reshape(
        token_count, KEY_HEADS, group_layout, HEAD_SIZE
    )
    local_keys = apply_rotation(
        matrix_product(first_normed, key_matrix).reshape(token_count, KEY_HEADS, HEAD_SIZE),
        cosine_table,
        sine_table,
    )
    local_keys = local_keys.astype(jnp.bfloat16).reshape(token_count, KEY_HEADS * HEAD_SIZE)
    values_own = matrix_product(first_normed, w_value).astype(jnp.bfloat16)
    gathered_keys, gathered_values = (
        lax.all_gather(local_keys, "shard", axis=0, tiled=True),
        lax.all_gather(values_own, "shard", axis=0, tiled=True),
    )
    gathered_keys = gathered_keys.reshape(device_group, KEY_HEADS, HEAD_SIZE)
    gathered_values = gathered_values.reshape(device_group, KEY_HEADS, HEAD_SIZE)

    def scores_of(key_value_head):
        raw = jnp.einsum(
            "tqd,sd->qts",
            query_rows[:, key_value_head],
            gathered_keys[:, key_value_head],
            preferred_element_type=jnp.float32,
        )
        return raw * score_scale

    head_outputs = []
    log_totals = []
    for key_value_head in range(KEY_HEADS):
        masked = jnp.where(allowed[None], scores_of(key_value_head), far_below)
        peak_score = jnp.max(masked, axis=-1, keepdims=True)
        weights = jnp.where(allowed[None], jnp.exp(masked - peak_score), 0.0)
        totals = jnp.sum(weights, axis=-1, keepdims=True)
        probabilities = weights / totals
        log_totals.append(peak_score + jnp.log(totals))
        head_outputs.append(
            jnp.einsum(
                "qts,sd->tqd",
                probabilities.astype(jnp.bfloat16),
                gathered_values[:, key_value_head],
                preferred_element_type=jnp.float32,
            )
        )
    attended = (
        jnp.stack(head_outputs, axis=1)
        .reshape(token_count, QUERY_HEADS * HEAD_SIZE)
        .astype(jnp.bfloat16)
    )
    middle = hidden + matrix_product(attended, w_out)
    gain_two, w_router, w_shared_up, w_shared_down, w_experts_up, w_experts_down = (
        lax.all_gather(g2, "shard", axis=0, tiled=True),
        lax.all_gather(wr, "shard", axis=0, tiled=True),
        lax.all_gather(w_su, "shard", axis=0, tiled=True),
        lax.all_gather(w_sd, "shard", axis=0, tiled=True),
        lax.all_gather(w_eu, "shard", axis=0, tiled=True),
        lax.all_gather(w_ed, "shard", axis=0, tiled=True),
    )
    unit_two, rms_two = norm_forward(middle)
    normed_two = (unit_two * gain_two.astype(jnp.float32)).astype(jnp.bfloat16)
    logits = matrix_product(normed_two, w_router)
    onehot = (expert_ids[:, :, None] == jnp.arange(EXPERTS, dtype=jnp.int32)[None, None, :]).astype(
        jnp.float32
    )
    chosen_mask = jnp.sum(onehot, axis=1)
    probs = jax.nn.softmax(logits, axis=-1)
    routed = chosen_mask * probs
    shared_both = matrix_product(normed_two, w_shared_up)
    shared_inner = silu_product(shared_both, SH).astype(jnp.bfloat16)
    summed_out = middle + matrix_product(shared_inner, w_shared_down)
    expert_boths = []
    expert_inners = []
    expert_results = []
    for expert in range(EXPERTS):
        both = matrix_product(normed_two, w_experts_up[:, expert])
        inner = silu_product(both, FF).astype(jnp.bfloat16)
        result = matrix_product(inner, w_experts_down[:, expert])
        summed_out = summed_out + routed[:, expert : expert + 1] * result
        expert_boths.append(both)
        expert_inners.append(inner)
        expert_results.append(result)
    mixed = summed_out.astype(jnp.bfloat16)
    upstream = cotangent.astype(jnp.float32)
    grad_shared_out = upstream.astype(jnp.bfloat16)
    grad_shared_inner = times_transposed(grad_shared_out, w_shared_down)
    grad_shared_both = swiglu_back(shared_both, grad_shared_inner, SH).astype(jnp.bfloat16)
    grad_normed = times_transposed(grad_shared_both, w_shared_up)
    shared_grads = reduce_grads(
        (weight_grad(normed_two, grad_shared_both), weight_grad(shared_inner, grad_shared_out))
    )
    up_grads = []
    down_grads = []
    routed_grads = []
    for expert in range(EXPERTS):
        grad_result = (routed[:, expert : expert + 1] * upstream).astype(jnp.bfloat16)
        routed_grads.append(jnp.sum(upstream * expert_results[expert], axis=-1))
        down_grads.append(weight_grad(expert_inners[expert], grad_result))
        grad_inner = times_transposed(grad_result, w_experts_down[:, expert])
        grad_both = swiglu_back(expert_boths[expert], grad_inner, FF).astype(jnp.bfloat16)
        up_grads.append(weight_grad(normed_two, grad_both))
        grad_normed = grad_normed + times_transposed(grad_both, w_experts_up[:, expert])
    grad_probs = chosen_mask * jnp.stack(routed_grads, axis=1)
    grad_logits = probs * (grad_probs - jnp.sum(probs * grad_probs, axis=-1, keepdims=True))
    grad_logits = grad_logits.astype(jnp.bfloat16)
    grad_router = weight_grad(normed_two, grad_logits)
    grad_normed = grad_normed + times_transposed(grad_logits, w_router)
    grad_middle_norm, grad_gain_two = norm_backward(grad_normed, unit_two, rms_two, gain_two)
    grad_middle = upstream + grad_middle_norm
    expert_grads = reduce_grads(
        (grad_gain_two, grad_router, jnp.stack(up_grads, axis=1), jnp.stack(down_grads, axis=1))
    )
    gain_one, w_query, key_matrix, w_value, w_out = fetch_attention()
    grad_proj_out = grad_middle.astype(jnp.bfloat16)
    grad_out_weight = weight_grad(attended, grad_proj_out)
    grad_attended = (
        times_transposed(grad_proj_out, w_out)
        .astype(jnp.bfloat16)
        .reshape(token_count, KEY_HEADS, group_layout, HEAD_SIZE)
    )
    query_grads = []
    key_gradients = []
    value_gradients = []
    for key_value_head in range(KEY_HEADS):
        scores = scores_of(key_value_head)
        probabilities = jnp.where(allowed[None], jnp.exp(scores - log_totals[key_value_head]), 0.0)
        grad_here = grad_attended[:, key_value_head]
        grad_weights = jnp.einsum(
            "tqd,sd->qts",
            grad_here,
            gathered_values[:, key_value_head],
            preferred_element_type=jnp.float32,
        )
        grad_scores = probabilities * (
            grad_weights - jnp.sum(probabilities * grad_weights, axis=-1, keepdims=True)
        )
        grad_scores = grad_scores.astype(jnp.bfloat16)
        query_grads.append(
            jnp.einsum(
                "qts,sd->tqd",
                grad_scores,
                gathered_keys[:, key_value_head],
                preferred_element_type=jnp.float32,
            )
            * score_scale
        )
        key_gradients.append(
            jnp.einsum(
                "qts,tqd->sd",
                grad_scores,
                query_rows[:, key_value_head],
                preferred_element_type=jnp.float32,
            )
            * score_scale
        )
        value_gradients.append(
            jnp.einsum(
                "qts,tqd->sd",
                probabilities.astype(jnp.bfloat16),
                grad_here,
                preferred_element_type=jnp.float32,
            )
        )
    reduced_keys, values_summed = (
        lax.psum_scatter(
            jnp.stack(key_gradients, axis=1)
            .reshape(device_group, KEY_HEADS * HEAD_SIZE)
            .astype(jnp.bfloat16),
            "shard",
            scatter_dimension=0,
            tiled=True,
        ).astype(jnp.float32),
        lax.psum_scatter(
            jnp.stack(value_gradients, axis=1)
            .reshape(device_group, KEY_HEADS * HEAD_SIZE)
            .astype(jnp.bfloat16),
            "shard",
            scatter_dimension=0,
            tiled=True,
        ).astype(jnp.float32),
    )
    grad_query = reverse_rotation(
        jnp.stack(query_grads, axis=1).reshape(token_count, QUERY_HEADS, HEAD_SIZE),
        cosine_table,
        sine_table,
    )
    grad_query = grad_query.reshape(token_count, QUERY_HEADS * HEAD_SIZE).astype(jnp.bfloat16)
    key_gradient = reverse_rotation(
        reduced_keys.reshape(token_count, KEY_HEADS, HEAD_SIZE), cosine_table, sine_table
    )
    key_gradient = key_gradient.reshape(token_count, KEY_HEADS * HEAD_SIZE).astype(jnp.bfloat16)
    grad_value = values_summed.astype(jnp.bfloat16)
    grad_normed_one = times_transposed(grad_query, w_query) + times_transposed(
        key_gradient, key_matrix
    )
    grad_normed_one = grad_normed_one + times_transposed(grad_value, w_value)
    grad_hidden_norm, grad_gain_one = norm_backward(grad_normed_one, unit_one, rms_one, gain_one)
    grad_of_input = (grad_middle + grad_hidden_norm).astype(jnp.bfloat16)
    attention_grads = reduce_grads(
        (
            grad_gain_one,
            weight_grad(first_normed, grad_query),
            weight_grad(first_normed, key_gradient),
            weight_grad(first_normed, grad_value),
            grad_out_weight,
        )
    )
    return (
        mixed,
        grad_of_input,
        attention_grads[0],
        attention_grads[1],
        attention_grads[2],
        attention_grads[3],
        attention_grads[4],
        expert_grads[0],
        expert_grads[1],
        shared_grads[0],
        shared_grads[1],
        expert_grads[2],
        expert_grads[3],
    )


MESH = pl.DeviceIdType.MESH


def neighbours():
    rank = lax.axis_index("replica")
    core = rank + 1 - 2 * (rank % 2)
    along_x = rank + 2 - 4 * ((rank // 2) % 2)
    along_y = rank + 4 - 8 * (rank // 4)
    return rank, core, along_x, along_y, along_x + along_y - rank


def greet(peers):
    barrier = pltpu.get_barrier_semaphore()
    for peer in peers:
        pl.semaphore_signal(barrier, inc=1, device_id=peer, device_id_type=MESH)
    pl.semaphore_wait(barrier, len(peers))


def send(src, dst, sends, recvs, at, peer):
    copy = pltpu.make_async_remote_copy(
        src_ref=src,
        dst_ref=dst,
        send_sem=sends.at[at],
        recv_sem=recvs.at[at],
        device_id=peer,
        device_id_type=MESH,
    )
    copy.start()
    return copy


class Relay:
    def __init__(self, source, block, width, odd, sends, recvs, at):
        rank, core, along_x, along_y, across = neighbours()
        here = lax.axis_index("shard")
        self.to_x, self.to_y, self.to_core = (along_x, here), (along_y, here), (core, here)
        self.rank, self.along_x, self.along_y, self.across = rank, along_x, along_y, across
        self.source, self.block, self.width = source, block, width
        self.cut = 128 * ((width // 128 + odd) // 2)
        self.sends, self.recvs, self.at = sends, recvs, at
        self.copies = []
        self.crossing = []

    def send(self, src, dst, k, peer):
        copy = send(src, dst, self.sends, self.recvs, (*self.at, k), peer)
        self.copies.append(copy)
        return copy

    def cross(self, src, dst, k):
        self.crossing.append(self.send(src, dst, k, self.to_core))

    def start(self):
        mine = self.block(self.rank, 0, self.width)
        self.over_x = self.send(self.source, mine, 0, self.to_x)
        self.over_y = self.send(self.source, mine, 1, self.to_y)
        self.cross(self.source, mine, 2)

    def middle(self):
        self.over_x.wait_recv()
        part = self.block(self.along_x, 0, self.cut)
        self.half_a = self.send(part, part, 3, self.to_y)
        self.over_y.wait_recv()
        part = self.block(self.along_y, self.cut, self.width)
        self.half_b = self.send(part, part, 4, self.to_x)
        for k, who in ((5, self.along_x), (6, self.along_y)):
            whole = self.block(who, 0, self.width)
            self.cross(whole, whole, k)

    def late(self):
        self.half_a.wait_recv()
        self.half_b.wait_recv()
        whole = self.block(self.across, 0, self.width)
        self.cross(whole, whole, 7)

    def finish(self):
        for copy in self.crossing:
            copy.wait_recv()
        for copy in self.copies:
            copy.wait_send()


def add_rows(dst, src):
    rows = dst.shape[0]
    size = 32 if rows % 32 == 0 else 16

    def body(step, _):
        at = pl.ds(pl.multiple_of(step * size, 16), size)
        dst[at, :] = dst[at, :] + src[at, :]
        return 0

    lax.fori_loop(0, rows // size, body, 0)


class Ring:
    def __init__(self, partial, full, make, buffers, semaphores):
        self.partial, self.full, self.make = partial, full, make
        self.right, self.left, self.own = buffers
        self.folds_s, self.folds_r, self.tells_s, self.tells_r, self.stays = semaphores
        self.rank = lax.axis_index("replica")
        self.here = lax.axis_index("shard")
        self.chunks, self.size = self.own.shape[0], self.own.shape[1]
        self.last = self.right.shape[1] - 1
        self.steps = self.chunks + 2 * self.last

    def prepare(self):
        @pl.when(self.here == 0)
        def _():
            for k in range(self.chunks):
                self.right[k, 0] = jnp.zeros(self.right.shape[2:], self.right.dtype)

        @pl.when(self.here == self.last)
        def _():
            for k in range(self.chunks):
                self.left[k, self.last] = jnp.zeros(self.left.shape[2:], self.left.dtype)

    def rows(self, b, k):
        first = (b * self.chunks + k) * self.size
        return pl.ds(pl.multiple_of(first, 16), self.size)

    def push(self, src, dst, sends, recvs, at, way):
        return pltpu.make_async_remote_copy(
            src_ref=src,
            dst_ref=dst,
            send_sem=sends.at[at],
            recv_sem=recvs.at[at],
            device_id=(self.rank, self.here + 1 - 2 * way),
            device_id_type=MESH,
        )

    def partial_copy(self, k, b, way, src=None):
        held = (self.right, self.left)[way].at[k, b]
        src = held if src is None else src
        return self.push(src, held, self.folds_s, self.folds_r, (way, k, b), way)

    def sides(self, b, way):
        inside = self.here < b if way == 0 else self.here > b
        edge = self.here == (0 if way == 0 else self.last)
        return inside, edge

    def lead(self, k):
        for way, blocks in ((0, range(self.last, 0, -1)), (1, range(self.last))):

            @pl.when(self.here == (0 if way == 0 else self.last))
            def _(way=way, blocks=blocks):
                for b in blocks:
                    self.partial_copy(k, b, way, self.partial.at[self.rows(b, k)]).start()

    def fold(self, i):
        for way, blocks in ((0, range(self.last, 0, -1)), (1, range(self.last))):
            k = i - self.here if way == 0 else i - self.last + self.here
            now = jnp.logical_and(k >= 0, k < self.chunks)
            for b in blocks:
                inside, edge = self.sides(b, way)
                inside = jnp.logical_and(inside, now)
                mine = self.partial.at[self.rows(b, k)]

                @pl.when(jnp.logical_and(inside, jnp.logical_not(edge)))
                def _(k=k, b=b, way=way, mine=mine):
                    copy = self.partial_copy(k, b, way)
                    copy.wait_recv()
                    add_rows((self.right, self.left)[way].at[k, b], mine)
                    copy.start()

    def settle(self, k):
        here = self.here

        @pl.when(here > 0)
        def _():
            self.partial_copy(k, here, 0).wait_recv()

        @pl.when(here < self.last)
        def _():
            self.partial_copy(k, here, 1).wait_recv()

        def part(step, _):
            inner = pl.ds(pl.multiple_of(step * 16, 16), 16)
            first = (here * self.chunks + k) * self.size + step * 16
            total = self.partial[pl.ds(pl.multiple_of(first, 16), 16), :].astype(jnp.float32)
            total = total + self.right[k, here, inner, :].astype(jnp.float32)
            total = total + self.left[k, here, inner, :].astype(jnp.float32)
            at = pl.ds(pl.multiple_of(k * self.size + step * 16, 16), 16)
            self.own[k, inner, :] = self.make(at, total)
            return 0

        lax.fori_loop(0, self.size // 16, part, 0)
        self.stay(k).start()
        for way in range(2):

            @pl.when(here < self.last if way == 0 else here > 0)
            def _(way=way):
                self.told(k, way).start()

    def stay(self, k):
        return pltpu.make_async_copy(
            self.own.at[k], self.full.at[self.rows(self.here, k)], self.stays.at[k]
        )

    def told(self, k, way):
        dst = self.full.at[self.rows(self.here, k)]
        return self.push(self.own.at[k], dst, self.tells_s, self.tells_r, (way, k, 0), way)

    def passed(self, k, way, hop, slot):
        block = self.here - hop if way == 0 else self.here + hop
        part = self.full.at[self.rows(block, k)]
        return self.push(part, part, self.tells_s, self.tells_r, (way, k, slot), way)

    def comes(self, way, hop):
        return self.here >= hop if way == 0 else self.here + hop <= self.last

    def goes_on(self, way, hop):
        return jnp.logical_and(
            self.comes(way, hop), self.here < self.last if way == 0 else self.here > 0
        )

    def forward(self, k, hop):
        for way in range(2):

            @pl.when(self.comes(way, hop))
            def _(way=way):
                self.passed(k, way, hop, hop - 1).wait_recv()

            if hop < self.last:

                @pl.when(self.goes_on(way, hop))
                def _(way=way):
                    self.passed(k, way, hop, hop).start()

    def step(self, i):
        if i == 0:
            self.lead(0)
        if i + 1 < self.chunks:
            self.lead(i + 1)
        if i < self.chunks + self.last:
            self.fold(i)
        if 0 <= i - self.last < self.chunks:
            self.settle(i - self.last)
        for hop in range(1, self.last + 1):
            if 0 <= i - self.last - hop < self.chunks:
                self.forward(i - self.last - hop, hop)

    def finish(self):
        for k in range(self.chunks):
            self.stay(k).wait()
            for way, blocks in ((0, range(self.last, 0, -1)), (1, range(self.last))):
                for b in blocks:
                    inside, _ = self.sides(b, way)

                    @pl.when(inside)
                    def _(k=k, b=b, way=way):
                        self.partial_copy(k, b, way).wait_send()

            for way in range(2):

                @pl.when(self.here < self.last if way == 0 else self.here > 0)
                def _(k=k, way=way):
                    self.told(k, way).wait_send()

                for hop in range(1, self.last):

                    @pl.when(self.goes_on(way, hop))
                    def _(k=k, way=way, hop=hop):
                        self.passed(k, way, hop, hop).wait_send()


def ring_scratch(group, planes_n, width, chunks):
    dma = pltpu.SemaphoreType.DMA
    size = group // planes_n // chunks
    return [
        pltpu.VMEM((chunks, planes_n, size, width), jnp.bfloat16),
        pltpu.VMEM((chunks, planes_n, size, width), jnp.bfloat16),
        pltpu.VMEM((chunks, size, width), jnp.bfloat16),
        dma((2, chunks, planes_n)),
        dma((2, chunks, planes_n)),
        dma((2, chunks, planes_n - 1)),
        dma((2, chunks, planes_n - 1)),
        dma((chunks,)),
    ]


def forward_norm(hidden, gain, middle, inverse):
    def make(at, total):
        total = total + hidden[at, :].astype(jnp.float32)
        rms = lax.rsqrt(jnp.mean(total * total, axis=-1, keepdims=True) + epsilon)
        middle[at, :] = total
        inverse[at, :] = jnp.broadcast_to(rms, (total.shape[0], inverse.shape[1]))
        return (total * rms * gain[...]).astype(jnp.bfloat16)

    return make


def backward_norm(cotangent, middle, inverse, gain, grad_middle, grad_gain):
    def make(at, total):
        rms = inverse[at, :1]
        unit = middle[at, :] * rms
        scaled = total * gain[...]
        grad = rms * (scaled - unit * jnp.mean(scaled * unit, axis=-1, keepdims=True))
        grad = grad + cotangent[at, :].astype(jnp.float32)
        grad_middle[at, :] = grad
        grad_gain[...] += jnp.sum(total * unit, axis=0, keepdims=True)
        return grad.astype(jnp.bfloat16)

    return make


def spread_kernel(items, sources, count, shared, ringed, *refs):
    ins, refs = refs[:sources], refs[sources:]
    if ringed:
        (partial, hidden, gain), refs = refs[:3], refs[3:]
    outs, refs = refs[:count], refs[count:]
    if ringed:
        (full, middle, inverse), refs = refs[:3], refs[3:]
    own, zs, zr, sends, recvs = refs[:5]
    ring = None
    if ringed:
        make = forward_norm(hidden, gain, middle, inverse)
        ring = Ring(partial, full, make, refs[5:8], refs[8:])
        ring.prepare()
    planes_n = 4
    piece = outs[0].shape[0] // 32
    rank, core, along_x, along_y, across = neighbours()
    here = lax.axis_index("shard")
    others = [(rank, (here + j) % planes_n) for j in range(1, planes_n)]
    greet(others + [(along_x, here), (along_y, here), (core, here)])

    def block(i, j, who, lo, hi):
        plane = (here + planes_n - j) % planes_n
        first = pl.multiple_of((plane * 8 + who) * piece, 16)
        return outs[i].at[pl.ds(first, piece), pl.ds(lo, hi - lo)]

    over_z, stays = {}, []
    for j in range(planes_n):
        target = (here + j) % planes_n
        for k, (src, whole, base, size, out, place) in enumerate(items):
            row = pl.multiple_of(rank * piece, 16) if whole else 0
            column = pl.multiple_of(base + target * size, 128)
            part = ins[src].at[pl.ds(row, piece), pl.ds(column, size)]
            dst = block(out, 0, rank, place, place + size)
            if j:
                over_z[j, k] = send(part, dst, zs, zr, (j, k), (rank, target))
            else:
                copy = pltpu.make_async_copy(part, dst, own.at[k])
                copy.start()
                stays.append(copy)
        if shared:
            src, dst = ins[-1], outs[-1].at[here]
            if j:
                over_z[j, len(items)] = send(
                    src, dst, zs, zr, (j, len(items)), (rank, target)
                )
            else:
                copy = pltpu.make_async_copy(src, dst, own.at[len(items)])
                copy.start()
                stays.append(copy)
    relays = []
    blocks = count - 1 if shared else count
    for j in range(planes_n):
        row = []
        for i in range(blocks):
            width = outs[i].shape[1]
            row.append(
                Relay(
                    block(i, j, rank, 0, width),
                    functools.partial(block, i, j),
                    width,
                    j % 2,
                    sends,
                    recvs,
                    (i, j),
                )
            )
        relays.append(row)
    starts = (0, 3, 5, 7) if ring else (0, 1, 2, 3)
    for step in range(max(starts[-1] + 3, ring.steps if ring else 0)):
        if ring and step < ring.steps:
            ring.step(step)
        for n, first in enumerate(starts):
            if step == first:
                if n == 0:
                    for copy in stays:
                        copy.wait()
                for (j, k), copy in over_z.items():
                    if j == n:
                        copy.wait_recv()
                for relay in relays[n]:
                    relay.start()
            if step == first + 1:
                for relay in relays[n]:
                    relay.middle()
            if step == first + 2:
                for relay in relays[n]:
                    relay.late()
    for copy in over_z.values():
        copy.wait_send()
    for row in relays:
        for relay in row:
            relay.finish()
    if ring:
        ring.finish()


def spread(ins, items, outs, shared, collective_id, micros, ring=None):
    dma = pltpu.SemaphoreType.DMA
    count = len(items) + (1 if shared else 0)
    any_space = pl.BlockSpec(memory_space=pl.ANY)
    vmem = pl.BlockSpec(memory_space=pltpu.VMEM)
    shaped = [jax.ShapeDtypeStruct(shape, jnp.bfloat16) for shape in outs]
    out_specs = [any_space] * len(outs)
    scratch = []
    if ring:
        group, tokens, width = ring[0].shape[0], ring[1].shape[0], ring[0].shape[1]
        shaped += [
            jax.ShapeDtypeStruct((group, width), jnp.bfloat16),
            jax.ShapeDtypeStruct((tokens, width), jnp.float32),
            jax.ShapeDtypeStruct((tokens, 128), jnp.float32),
        ]
        out_specs += [any_space, vmem, vmem]
        scratch = ring_scratch(group, group // tokens, width, 8)
    return pl.pallas_call(
        functools.partial(spread_kernel, items, len(ins), len(outs), shared, ring is not None),
        out_shape=shaped,
        in_specs=[any_space] * len(ins) + ([vmem] * 3 if ring else []),
        out_specs=out_specs,
        scratch_shapes=[dma((count,))]
        + [dma((4, count))] * 2
        + [dma((len(outs), 4, 8))] * 2
        + scratch,
        compiler_params=pltpu.CompilerParams(
            collective_id=collective_id, has_side_effects=True, vmem_limit_bytes=32 * 2**20
        ),
        cost_estimate=pl.CostEstimate(
            flops=0, bytes_accessed=int(micros * 3.0e6), transcendentals=0
        ),
    )(*ins, *(ring or ()))


class Fold:
    def __init__(self, factor, plane, slot, buffers, j, sends, recvs, at):
        rank, core, along_x, along_y, _ = neighbours()
        here = lax.axis_index("shard")
        self.c, self.x, self.y = rank % 2, (rank // 2) % 2, rank // 4
        self.to_x, self.to_y, self.to_core = (along_x, here), (along_y, here), (core, here)
        self.left, self.left_first, self.right, self.right_first = factor
        self.plane, self.mine, self.before = plane, slot, None
        self.held, self.far_a, self.far_b, self.near_a, self.near_b = [b.at[j] for b in buffers]
        self.cut, self.rest = self.near_a.shape[1], self.near_b.shape[1]
        self.sends, self.recvs, self.at = sends, recvs, at
        self.copies = []

    def send(self, src, dst, k, peer):
        copy = send(src, dst, self.sends, self.recvs, (self.at, k), peer)
        self.copies.append(copy)
        return copy

    def begin(self):
        _, _, _, m, n = self.mine.shape
        column = pl.multiple_of(self.left_first + self.plane * 8 * m, 128)
        tile = 512 if n % 512 == 0 else n
        if self.before is not None:
            self.before.first.wait_send()
            self.before.copies.remove(self.before.first)

        def product(step, _):
            at = pl.ds(pl.multiple_of(step * tile, 128), tile)
            there = pl.ds(pl.multiple_of(self.right_first + step * tile, 128), tile)
            block = over_first(self.left[:, pl.ds(column, 8 * m)], self.right[:, there])
            block = block.astype(self.mine.dtype)
            for r in range(8):
                self.mine[r // 4, (r // 2) % 2, r % 2, :, at] = block[r * m : (r + 1) * m, :]
            return 0

        lax.fori_loop(0, n // tile, product, 0)
        self.first = self.send(self.mine.at[:, :, 1 - self.c], self.held, 0, self.to_core)

    def start(self):
        self.first.wait_recv()
        for p in range(2):
            for q in range(2):
                add_rows(self.held.at[p, q], self.mine.at[p, q, self.c])
        left, right = pl.ds(0, self.cut), pl.ds(self.cut, self.rest)
        self.over_x = self.send(self.held.at[:, 1 - self.x, :, left], self.far_a, 1, self.to_x)
        self.over_y = self.send(self.held.at[1 - self.y, :, :, right], self.far_b, 2, self.to_y)

    def middle(self):
        left, right = pl.ds(0, self.cut), pl.ds(self.cut, self.rest)
        self.over_x.wait_recv()
        for p in range(2):
            add_rows(self.far_a.at[p], self.held.at[p, self.x, :, left])
        self.last_a = self.send(self.far_a.at[1 - self.y], self.near_a, 3, self.to_y)
        self.over_y.wait_recv()
        for q in range(2):
            add_rows(self.far_b.at[q], self.held.at[self.y, q, :, right])
        self.last_b = self.send(self.far_b.at[1 - self.x], self.near_b, 4, self.to_x)

    def late(self):
        self.last_a.wait_recv()
        add_rows(self.near_a, self.far_a.at[self.y])
        self.last_b.wait_recv()
        add_rows(self.near_b, self.far_b.at[self.x])

    def finish(self):
        for copy in self.copies:
            copy.wait_send()


def exchange_kernel(setup, *refs):
    shapes, factors, plans, after, counts = setup
    operands_n, ring_n, sources_n, tiny, out_count, slot_keys = counts
    count = len(shapes)

    def take(number):
        nonlocal refs
        head, refs = refs[:number], refs[number:]
        return head

    operands, ring_in, sources = take(operands_n), take(ring_n), take(sources_n)
    tiny_in = take(tiny)
    outs, wide, later = take(out_count), take(sources_n), take(len(after))
    tiny_outs = take(2 * tiny)
    ring_out = take(3 if ring_n else 0)
    slots = dict(zip(slot_keys, take(len(slot_keys))))
    sets = [take(5) for _ in range(count)]
    sends, recvs, own, zs, zr, relay_sends, relay_recvs, relay_own, tiny_s, tiny_r, tiny_own = take(11)
    ring = None
    if ring_n:
        partial, cotangent, middle, inverse, gain = ring_in
        full, grad_middle, grad_gain = ring_out
        make = backward_norm(cotangent, middle, inverse, gain, grad_middle, grad_gain)
        ring = Ring(partial, full, make, refs[:3], refs[3:])
        ring.prepare()
        grad_gain[...] = jnp.zeros_like(grad_gain)
    rank, core, along_x, along_y, _ = neighbours()
    here = lax.axis_index("shard")
    planes_n = 4
    peers = [(along_x, here), (along_y, here), (core, here)]
    greet(peers + [(rank, (here + j) % planes_n) for j in range(1, planes_n)])
    tiny_copies = []
    for ref in tiny_in:
        m = ref.shape[1]
        for j in range(planes_n):
            target = (here + j) % planes_n
            dst = tiny_outs[0].at[pl.ds(pl.multiple_of(here * m, 8), m)]
            if j:
                copy = send(ref.at[target], dst, tiny_s, tiny_r, (j,), (rank, target))
            else:
                copy = pltpu.make_async_copy(ref.at[here], dst, tiny_own.at[0])
                copy.start()
            tiny_copies.append(copy)

    folds = []
    settled = {}
    used = {}
    for i, (a, m, n) in enumerate(shapes):
        left, left_first, right, right_first = factors[i]
        factor = (operands[left], left_first, operands[right], right_first)
        for j in list(range(1, a)) + [0]:
            plane = (here + j) % planes_n if a > 1 else 0
            users = used.setdefault((m, n), [])
            depth = slots[m, n].shape[0]
            slot = slots[m, n].at[len(users) % depth]
            piece = Fold(factor, plane, slot, sets[i], j, sends, recvs, len(folds))
            if len(users) >= depth:
                piece.before = users[-depth]
            users.append(piece)
            for plan in plans[i]:
                settled[plan[2]] = len(folds) + 2
            folds.append((i, j, piece))
    finals = {k: [] for k in range(out_count)}

    def settle(chunk, n):
        i, j, piece = chunk
        for half, (buf, lo, hi) in enumerate(
            (
                (piece.near_a, 0, piece.cut),
                (piece.near_b, piece.cut, piece.cut + piece.rest),
            )
        ):
            for k, (offset, size, out, base, top) in enumerate(plans[i]):
                left, right = max(lo, offset), min(hi, offset + size)
                if left >= right:
                    continue
                src = buf.at[:, pl.ds(left - lo, right - left)]
                place = base + (left - offset)
                if shapes[i][0] > 1:
                    place = pl.multiple_of(place + here * size, 128)
                dst = outs[out].at[pl.ds(top, shapes[i][1]), pl.ds(place, right - left)]
                if j == 0:
                    copy = pltpu.make_async_copy(src, dst, own.at[n, 2 * k + half])
                    copy.start()
                else:
                    target = (rank, (here + j) % planes_n)
                    copy = send(src, dst, zs, zr, (i, j, 2 * k + half), target)
                finals[out].append(copy)

    relays = []
    total = len(folds) + 2 if folds else 0

    def add_relays(source, out, ready, waits):
        nonlocal total
        m, n = source.shape
        for lo in range(0, n, 1536):
            hi = min(n, lo + 1536)

            def block(who, left, right, lo=lo):
                first = pl.multiple_of(who * m, 16)
                return out.at[pl.ds(first, m), pl.ds(lo + left, right - left)]

            number = len(relays)
            part = source.at[:, pl.ds(lo, hi - lo)]
            relay = Relay(part, block, hi - lo, number % 2, relay_sends, relay_recvs, (number,))
            stay = pltpu.make_async_copy(part, block(relay.rank, 0, hi - lo), relay_own.at[number])
            start = max(ready, relays[-1][0] + 1 if relays else 0)
            relays.append((start, relay, stay, waits if lo == 0 else []))
            total = max(total, start + 3)

    for source, out in zip(sources, wide):
        add_relays(source, out, 0, [])
    for n in sorted(range(len(after)), key=lambda n: settled[after[n]]):
        add_relays(outs[after[n]], later[n], settled[after[n]], finals[after[n]])
    if tiny:
        add_relays(tiny_outs[0], tiny_outs[1], 1, tiny_copies)
    if ring:
        total = max(total, ring.steps)
    if folds:
        folds[0][2].begin()
    for step in range(total):
        if step < len(folds):
            folds[step][2].start()
        if step + 1 < len(folds):
            folds[step + 1][2].begin()
        if 0 <= step - 1 < len(folds):
            folds[step - 1][2].middle()
        if 0 <= step - 2 < len(folds):
            folds[step - 2][2].late()
            settle(folds[step - 2], step - 2)
        for start, relay, stay, waits in relays:
            if step == start:
                for copy in waits:
                    copy.wait()
                relay.start()
                stay.start()
            elif step == start + 1:
                relay.middle()
            elif step == start + 2:
                relay.late()
        if ring and step < ring.steps:
            ring.step(step)
    relayed = list(after)
    for out, copies in finals.items():
        if out not in relayed:
            for copy in copies:
                copy.wait()
    for _, relay, stay, _ in relays:
        relay.finish()
        stay.wait()
    for _, _, piece in folds:
        piece.finish()
    if ring:
        ring.finish()


def exchange(
    operands, factors, shapes, plans, outs, sources, after, collective_id, micros, tiny=None, ring=()
):
    dma = pltpu.SemaphoreType.DMA
    bf16, f32 = jnp.bfloat16, jnp.float32
    any_space = pl.BlockSpec(memory_space=pl.ANY)
    vmem = pl.BlockSpec(memory_space=pltpu.VMEM)
    keys = {}
    for a, m, n in shapes:
        keys[m, n] = keys.get((m, n), 0) + a
    scratch = [pltpu.VMEM((min(2, number), 2, 2, 2, *key), bf16) for key, number in keys.items()]
    for a, m, n in shapes:
        cut = 128 * (n // 256)
        scratch += [
            pltpu.VMEM((a, 2, 2, m, n), bf16),
            pltpu.VMEM((a, 2, m, cut), bf16),
            pltpu.VMEM((a, 2, m, n - cut), bf16),
            pltpu.VMEM((a, m, cut), bf16),
            pltpu.VMEM((a, m, n - cut), bf16),
        ]
    total = max(1, sum(shape[0] for shape in shapes))
    most = 2 * max([len(plan) for plan in plans] + [1])
    deep = max([shape[0] for shape in shapes] + [1])
    widths = [s.shape[1] for s in sources] + [outs[k][1] for k in after]
    relays = 1 + sum(-(-w // 1536) for w in widths)
    wide = [(8 * s.shape[0], s.shape[1]) for s in sources]
    later = [(8 * outs[k][0], outs[k][1]) for k in after]
    shaped = [jax.ShapeDtypeStruct(shape, bf16) for shape in outs + wide + later]
    extras = []
    if tiny is not None:
        planes_n, m, n = tiny.shape
        extras = [tiny]
        shaped += [
            jax.ShapeDtypeStruct((planes_n * m, n), tiny.dtype),
            jax.ShapeDtypeStruct((8 * planes_n * m, n), tiny.dtype),
        ]
    specs = [any_space] * len(shaped)
    scratch += [dma((total, 5))] * 2 + [dma((total, most))]
    scratch += [dma((max(1, len(shapes)), deep, most))] * 2
    scratch += [dma((relays, 8))] * 2 + [dma((relays,))]
    scratch += [dma((4,))] * 2 + [dma((1,))]
    if ring:
        group, tokens, width = ring[0].shape[0], ring[1].shape[0], ring[0].shape[1]
        shaped += [
            jax.ShapeDtypeStruct((group, width), bf16),
            jax.ShapeDtypeStruct((tokens, width), f32),
            jax.ShapeDtypeStruct((1, width), f32),
        ]
        specs += [any_space, vmem, vmem]
        scratch += ring_scratch(group, group // tokens, width, 8)
    counts = (len(operands), len(ring), len(sources), len(extras), len(outs), list(keys))
    results = pl.pallas_call(
        functools.partial(exchange_kernel, (shapes, factors, plans, after, counts)),
        out_shape=shaped,
        in_specs=[vmem] * (len(operands) + len(ring)) + [any_space] * (len(sources) + len(extras)),
        out_specs=specs,
        scratch_shapes=scratch,
        compiler_params=pltpu.CompilerParams(
            collective_id=collective_id, has_side_effects=True, vmem_limit_bytes=60 * 2**20
        ),
        cost_estimate=pl.CostEstimate(
            flops=0, bytes_accessed=int(micros * 3.0e6), transcendentals=0
        ),
    )(*operands, *ring, *sources, *extras)
    return results[: len(outs)], results[len(outs) :]


def turn(entries, cosines, sines):
    return entries * cosines + pltpu.roll(entries, HEAD_SIZE // 2, 1) * sines


def readable(begin, first, size, keys):
    place = lax.broadcasted_iota(jnp.int32, (size, keys), 0) + first
    key = lax.broadcasted_iota(jnp.int32, (size, keys), 1)
    return (key >= begin) & (key <= place)


def over_last(left, right):
    return lax.dot_general(
        left, right, (((1,), (1,)), ((), ())), preferred_element_type=jnp.float32
    )


def over_first(left, right):
    return lax.dot_general(
        left, right, (((0,), (0,)), ((), ())), preferred_element_type=jnp.float32
    )


def attend_kernel(x, gain, w, wo, cosines, sines, begin, n1, inverse, q, k, v, o, lse, out):
    f32, bf16 = jnp.float32, jnp.bfloat16
    group, width = x.shape
    heads = q.shape[1] // HEAD_SIZE
    size = 128
    scale = HEAD_SIZE ** (-0.5)

    def norm(step, _):
        at = pl.ds(pl.multiple_of(step * 64, 64), 64)
        rows = x[at, :].astype(f32)
        rms = lax.rsqrt(jnp.mean(rows * rows, axis=-1, keepdims=True) + epsilon)
        inverse[at, :] = jnp.broadcast_to(rms, (64, inverse.shape[1]))
        n1[at, :] = (rows * rms * gain[...]).astype(bf16)
        return 0

    lax.fori_loop(0, group // 64, norm, 0)
    for h in range(heads + 1):
        at = slice(h * HEAD_SIZE, (h + 1) * HEAD_SIZE)
        both = matrix_product(n1[...], w[:, at])
        turned = turn(both, cosines[...], sines[...]).astype(bf16)
        if h < heads:
            q[:, at] = turned
        else:
            k[...] = turned
    v[...] = matrix_product(n1[...], w[:, (heads + 1) * HEAD_SIZE :]).astype(bf16)
    for i in range(group // size):
        rows = slice(i * size, (i + 1) * size)
        keys = (i + 1) * size
        allowed = readable(begin[rows, :], i * size, size, keys)
        lane = lax.broadcasted_iota(jnp.int32, (size, HEAD_SIZE), 1)
        logs = jnp.zeros((size, HEAD_SIZE), f32)
        for h in range(heads):
            at = slice(h * HEAD_SIZE, (h + 1) * HEAD_SIZE)
            scores = over_last(q[rows, at], k[:keys, :]) * scale
            scores = jnp.where(allowed, scores, far_below)
            peak = jnp.max(scores, axis=-1, keepdims=True)
            weights = jnp.exp(scores - peak)
            total = jnp.sum(weights, axis=-1, keepdims=True)
            probs = (weights / total).astype(bf16)
            logs = jnp.where(lane == h, peak + jnp.log(total), logs)
            o[rows, at] = matrix_product(probs, v[:keys, :]).astype(bf16)
        lse[rows, :] = logs

    def project(step, _):
        at = pl.ds(pl.multiple_of(step * 512, 512), 512)
        out[:, at] = matrix_product(o[...], wo[:, at]).astype(bf16)
        return 0

    lax.fori_loop(0, width // 512, project, 0)


def attend(x, gain, w, wo, cosines, sines, begin):
    f32, bf16 = jnp.float32, jnp.bfloat16
    group, width = x.shape
    q_width = w.shape[1] - 2 * HEAD_SIZE
    shaped = [
        ((group, width), bf16),
        ((group, HEAD_SIZE), f32),
        ((group, q_width), bf16),
        ((group, HEAD_SIZE), bf16),
        ((group, HEAD_SIZE), bf16),
        ((group, q_width), bf16),
        ((group, HEAD_SIZE), f32),
        ((group, width), bf16),
    ]
    return pl.pallas_call(
        attend_kernel,
        out_shape=[jax.ShapeDtypeStruct(*s) for s in shaped],
        compiler_params=pltpu.CompilerParams(vmem_limit_bytes=48 * 2**20),
        cost_estimate=pl.CostEstimate(flops=0, bytes_accessed=60000000, transcendentals=0),
    )(x, gain, w, wo, cosines, sines, begin)


def attend_back_kernel(
    dm, wo, x, inverse, q, k, v, lse, w, cosines, sines, begin, dqkv, dn1, dgain, dk, dv
):
    f32, bf16 = jnp.float32, jnp.bfloat16
    group, width = dm.shape
    heads = q.shape[1] // HEAD_SIZE
    size = 128
    scale = HEAD_SIZE ** (-0.5)
    dk[...] = jnp.zeros_like(dk)
    dv[...] = jnp.zeros_like(dv)
    for h in range(heads):
        at = slice(h * HEAD_SIZE, (h + 1) * HEAD_SIZE)
        upstream = over_last(dm[...], wo[at, :]).astype(bf16)
        for i in range(group // size):
            rows = slice(i * size, (i + 1) * size)
            keys = (i + 1) * size
            allowed = readable(begin[rows, :], i * size, size, keys)
            scores = over_last(q[rows, at], k[:keys, :]) * scale
            probs = jnp.where(allowed, jnp.exp(scores - lse[rows, h : h + 1]), 0.0)
            grad = over_last(upstream[rows, :], v[:keys, :])
            grad = probs * (grad - jnp.sum(probs * grad, axis=-1, keepdims=True))
            grad = grad.astype(bf16)
            dq = matrix_product(grad, k[:keys, :]) * scale
            dqkv[rows, at] = turn(dq, cosines[rows, :], -sines[rows, :]).astype(bf16)
            dk[:keys, :] += over_first(grad, q[rows, at])
            dv[:keys, :] += over_first(probs.astype(bf16), upstream[rows, :])
    at = slice(heads * HEAD_SIZE, (heads + 1) * HEAD_SIZE)
    dqkv[:, at] = turn(dk[...] * scale, cosines[...], -sines[...]).astype(bf16)
    dqkv[:, (heads + 1) * HEAD_SIZE :] = dv[...].astype(bf16)

    def project(step, _):
        at = pl.ds(pl.multiple_of(step * 256, 256), 256)
        grad = over_last(dqkv[...], w[at, :])
        dn1[:, at] = grad.astype(bf16)
        unit = x[:, at].astype(f32) * inverse[:, :1]
        dgain[:, at] = jnp.sum(grad * unit, axis=0, keepdims=True)
        return 0

    lax.fori_loop(0, width // 256, project, 0)


def attend_back(dm, wo, x, inverse, q, k, v, lse, w, cosines, sines, begin):
    f32, bf16 = jnp.float32, jnp.bfloat16
    group, width = x.shape
    shaped = [((group, w.shape[1]), bf16), ((group, width), bf16), ((1, width), f32)]
    return pl.pallas_call(
        attend_back_kernel,
        out_shape=[jax.ShapeDtypeStruct(*s) for s in shaped],
        scratch_shapes=[pltpu.VMEM((group, HEAD_SIZE), f32)] * 2,
        compiler_params=pltpu.CompilerParams(vmem_limit_bytes=48 * 2**20),
        cost_estimate=pl.CostEstimate(flops=0, bytes_accessed=75000000, transcendentals=0),
    )(dm, wo, x, inverse, q, k, v, lse, w, cosines, sines, begin)


def widen_kernel(groups, scattered, order, *refs):
    results = refs[sum(8 if many else 1 for many in scattered) :]

    def write(source, group, at):
        for first, rows, column, size, parts, along_rows in group:
            out = results[at]
            at += 1
            for e in range(parts):
                top = first + (e * rows if along_rows else 0)
                left = column + (0 if along_rows else e * size)
                block = source[pl.ds(top, rows), pl.ds(left, size)].astype(out.dtype)
                if parts == 1:
                    out[...] = block
                else:
                    out[:, e, :] = block

    at = 0
    for group, many in zip(groups, scattered):
        if many:
            for n in range(8):

                @pl.when(order[pl.program_id(0)] == n)
                def _(source=refs[n], group=group, at=at):
                    write(source, group, at)

        else:
            write(refs[0], group, at)
        refs = refs[8 if many else 1 :]
        at += len(group)


def widen(sources, groups, order):
    steps = order.shape[0]
    out_shape, out_specs, in_specs, flat, scattered = [], [], [], [], []
    for group in groups:
        for _, rows, _, size, parts, _ in group:
            if parts == 1:
                out_shape.append(jax.ShapeDtypeStruct((steps * rows, size), jnp.float32))
                out_specs.append(pl.BlockSpec((rows, size), lambda i, order: (i, 0)))
            else:
                out_shape.append(jax.ShapeDtypeStruct((steps * rows, parts, size), jnp.float32))
                out_specs.append(pl.BlockSpec((rows, parts, size), lambda i, order: (i, 0, 0)))
    for s in sources:
        many = isinstance(s, list)
        scattered.append(many)
        for part in s if many else [s]:
            flat.append(part)
            if many:
                in_specs.append(pl.BlockSpec(part.shape, lambda i, order: (0, 0)))
            else:
                block = (part.shape[0] // steps, part.shape[1])
                in_specs.append(pl.BlockSpec(block, lambda i, order: (i, 0)))
    return pl.pallas_call(
        functools.partial(widen_kernel, groups, scattered),
        grid_spec=pltpu.PrefetchScalarGridSpec(
            num_scalar_prefetch=1, grid=(steps,), in_specs=in_specs, out_specs=out_specs
        ),
        out_shape=out_shape,
        compiler_params=pltpu.CompilerParams(vmem_limit_bytes=56 * 2**20),
        cost_estimate=pl.CostEstimate(
            flops=0, bytes_accessed=sum(6 * f.size for f in flat), transcendentals=0
        ),
    )(order, *flat)


def share_out(block, cut, between=None):
    def swap(x, bit):
        return lax.ppermute(x, "replica", [(i, i ^ bit) for i in range(8)])

    along_x, along_y = swap(block, 2), swap(block, 4)
    if between is not None:
        along_x, along_y = between(along_x, along_y)
    far = [swap(x, 1) for x in (block, along_x, along_y)]
    across = jnp.concatenate([swap(along_x[:, :cut], 4), swap(along_y[:, cut:], 2)], axis=1)
    far.append(swap(across, 1))
    return [x for pair in zip((block, along_x, along_y, across), far) for x in pair]


def planes(
    layer_input, cotangent, lengths, expert_ids, g1, wq, wk, wv, wo, g2, wr, w_su, w_sd, w_eu, w_ed
):
    tokens, width = layer_input.shape
    count = lax.axis_size("shard")
    copies = lax.axis_size("replica")
    rows = wq.shape[0]
    piece = rows // copies
    group = tokens * count
    heads = QUERY_HEADS // count
    sh, ff = SH // count, FF // count
    scale = HEAD_SIZE ** (-0.5)
    f32, bf16 = jnp.float32, jnp.bfloat16
    q_width = heads * HEAD_SIZE
    rank = lax.axis_index("replica")
    kv_width = KEY_HEADS * HEAD_SIZE

    def all_tokens(x):
        return lax.all_gather(x, "shard", axis=0, tiled=True)

    def own_tokens(x):
        return lax.psum_scatter(x, "shard", scatter_dimension=0, tiled=True).astype(f32)

    hidden_all = all_tokens(layer_input)
    flags = jnp.pad(expert_ids.reshape(1, tokens).astype(bf16), ((0, 0), (0, rows - tokens)))
    small = jnp.concatenate([g1[None], g2[None], wr.T, flags, jnp.zeros((11, rows), bf16)], axis=0)
    w_qkv, small = spread(
        [wq, wk, wv, small],
        [
            (0, True, 0, q_width, 0, 0),
            (1, True, 0, HEAD_SIZE, 0, q_width),
            (2, True, 0, HEAD_SIZE, 0, q_width + HEAD_SIZE),
        ],
        [(width, q_width + 2 * HEAD_SIZE), (count, 16, rows)],
        True,
        1,
        40,
    )
    gain_one, gain_two = small[:, 0].reshape(width), small[:, 1].reshape(width)
    w_router = small[:, 2 : 2 + EXPERTS].transpose(1, 0, 2).reshape(EXPERTS, width)
    ids = small[:, 2 + EXPERTS, :tokens].reshape(group, 1).astype(jnp.int32)
    cot, w_qkv = lax.optimization_barrier((cotangent, w_qkv))
    upstream = all_tokens(cot)
    w_ed_rows = [w_ed[:, e] for e in range(EXPERTS)]
    mine_eu = lax.dynamic_slice_in_dim(w_eu, rank * piece, piece, axis=0)
    mine_eu = [mine_eu[:, e] for e in range(EXPERTS)]

    _, position = layout(lengths[0], group)
    begin = (jnp.arange(group, dtype=jnp.int32) - position)[:, None]
    cosine_table, sine_table = angles(position)
    cosines = jnp.concatenate([cosine_table, cosine_table], axis=1)
    sines = jnp.concatenate([-sine_table, sine_table], axis=1)
    hidden = layer_input.astype(f32)
    n1, inverse, q, k, v, attended, lse, partial_wo = attend(
        hidden_all, gain_one.astype(f32)[None], w_qkv, wo, cosines, sines, begin
    )
    up_items = [(0, True, 0, sh, 0, 0), (0, True, SH, sh, 0, sh)]
    for e in range(EXPERTS):
        for half in range(2):
            up_items.append((1 + e, False, half * FF, ff, 0, 2 * sh + (2 * e + half) * ff))
    partial_wo, w_su_now = lax.optimization_barrier((partial_wo, w_su))
    w_up, n2, middle, inverse_two = spread(
        [w_su_now, *mine_eu],
        up_items,
        [(width, 2 * sh + 2 * EXPERTS * ff)],
        False,
        2,
        110,
        ring=(partial_wo, layer_input, gain_two.astype(f32)[None]),
    )
    logits = times_transposed(n2, w_router)
    chosen = jnp.sum(
        (ids[:, :, None] == jnp.arange(EXPERTS, dtype=jnp.int32)[None, None, :]).astype(f32), axis=1
    )
    probs = jax.nn.softmax(logits, axis=-1)
    routed = chosen * probs
    z = matrix_product(n2, w_up)
    factor = jnp.concatenate(
        [jnp.ones((group, sh), f32)]
        + [jnp.broadcast_to(routed[:, e : e + 1], (group, ff)) for e in range(EXPERTS)],
        axis=1,
    )
    gate = jnp.concatenate(
        [z[:, :sh]] + [z[:, 2 * sh + 2 * e * ff :][:, :ff] for e in range(EXPERTS)], axis=1
    )
    up = jnp.concatenate(
        [z[:, sh : 2 * sh]] + [z[:, 2 * sh + (2 * e + 1) * ff :][:, :ff] for e in range(EXPERTS)],
        axis=1,
    )
    sigma = jax.nn.sigmoid(gate)
    inner = gate * sigma * up
    inner_low = (factor * inner).astype(bf16)
    down_parts = [w_sd] + w_ed_rows
    spans = [slice(0, sh)] + [slice(sh + e * ff, sh + (e + 1) * ff) for e in range(EXPERTS)]
    grad_inner = jnp.concatenate([times_transposed(upstream, w) for w in down_parts], axis=1)
    kept = inner * grad_inner
    routed_grads = jnp.stack([jnp.sum(kept[:, span], axis=-1) for span in spans[1:]], axis=1)
    scaled = factor * grad_inner
    grad_gate = (scaled * up * sigma * (1.0 + gate * (1.0 - sigma))).astype(bf16)
    grad_up = (scaled * gate * sigma).astype(bf16)
    pieces = []
    for span in spans:
        pieces += [grad_gate[:, span], grad_up[:, span]]
    grad_z = jnp.concatenate(pieces, axis=1)
    grad_probs = chosen * routed_grads
    grad_logits = probs * (grad_probs - jnp.sum(probs * grad_probs, axis=-1, keepdims=True))
    grad_logits = grad_logits.astype(bf16)
    grad_n2 = times_transposed(grad_z, w_up) + matrix_product(grad_logits, w_router)
    grad_router = weight_grad(grad_logits, n2)
    down_rows = [w.shape[0] // copies for w in down_parts]
    down_tops = [sum(down_rows[:i]) for i in range(len(down_rows))]
    plan_su = [(0, sh, 1, 0, 0), (sh, sh, 1, SH, 0)]
    plan_eu = [(n * ff, ff, 2, n * FF, 0) for n in range(2 * EXPERTS)]
    (_, _, eu_share), (down_all, su_all, grad_proj, grad_middle, grad_gain_two) = exchange(
        [inner_low, upstream, n2, grad_z],
        [(0, spans[1].start, 1, 0), (2, 0, 3, 0), (2, 0, 3, 2 * sh)]
        + [(0, span.start, 1, 0) for span in [spans[0]] + spans[2:]],
        [(1, down_rows[1], width), (count, piece, 2 * sh), (count, piece, 2 * EXPERTS * ff)]
        + [(1, n, width) for n in [down_rows[0]] + down_rows[2:]],
        [[(0, width, 0, 0, down_tops[1])], plan_su, plan_eu]
        + [[(0, width, 0, 0, top)] for top in [down_tops[0]] + down_tops[2:]],
        [(sum(down_rows), width), (piece, 2 * SH), (piece, 2 * EXPERTS * FF)],
        [],
        [0, 1],
        3,
        180,
        ring=(grad_n2.astype(bf16), cotangent, middle, inverse_two, gain_two.astype(f32)[None]),
    )
    grad_proj, inner_low = lax.optimization_barrier((grad_proj, inner_low))
    order = jnp.bitwise_xor(jnp.arange(copies, dtype=jnp.int32), rank)
    eu_all = share_out(eu_share, EXPERTS * FF)
    grad_qkv, grad_n1, grad_gain_one = attend_back(
        grad_proj, wo, hidden_all, inverse, q, k, v, lse, w_qkv, cosines, sines, begin
    )
    tiny = jnp.concatenate(
        [grad_gain_one, grad_gain_two, grad_router, jnp.zeros((4, width), f32)], axis=0
    )
    tiny = tiny.reshape(8, count, rows).transpose(1, 0, 2)
    grad_n1, grad_qkv = lax.optimization_barrier((grad_n1, grad_qkv))
    grad_n1 = own_tokens(grad_n1)
    partial_out = sum(
        matrix_product(inner_low[:, span], w) for span, w in zip(spans, down_parts)
    )
    mixed = (middle + own_tokens(partial_out.astype(bf16))).astype(bf16)
    plan_qkv = [
        (0, q_width, 0, width, 0),
        (q_width, HEAD_SIZE, 0, 2 * width, 0),
        (q_width + HEAD_SIZE, HEAD_SIZE, 0, 2 * width + kv_width, 0),
    ]
    (share,), (_, tiny) = exchange(
        [attended, grad_proj, n1, grad_qkv],
        [(2, 0, 3, 0), (0, 0, 1, 0)],
        [(count, piece, q_width + 2 * HEAD_SIZE), (1, piece, width)],
        [plan_qkv, [(0, width, 0, 0, 0)]],
        [(piece, 2 * width + 2 * kv_width)],
        [],
        [],
        5,
        45,
        tiny=tiny,
    )
    share, down_all, su_all = lax.optimization_barrier((share, down_all, su_all))
    mlp_grads = widen(
        [down_all, su_all, eu_all],
        [
            [
                (0, down_rows[0], 0, width, 1, True),
                (down_rows[0], down_rows[1], 0, width, EXPERTS, True),
            ],
            [(0, piece, 0, 2 * SH, 1, True)],
            [(0, piece, 0, 2 * FF, EXPERTS, False)],
        ],
        order,
    )

    def beside(*blocks):
        nonlocal mlp_grads
        *blocks, mlp_grads = lax.optimization_barrier((*blocks, mlp_grads))
        return blocks

    att_all = share_out(share, EXPERTS * FF, beside)
    sd_grad, ed_grad, su_grad, eu_grad = mlp_grads
    wo_grad, wq_grad, wk_grad, wv_grad = widen(
        [att_all],
        [
            [
                (0, piece, 0, width, 1, True),
                (0, piece, width, width, 1, True),
                (0, piece, 2 * width, kv_width, 1, True),
                (0, piece, 2 * width + kv_width, kv_width, 1, True),
            ],
        ],
        order,
    )
    tiny = jnp.sum(tiny.reshape(copies * count, 8, rows), axis=0)
    unit_one, rms_one = norm_forward(hidden)
    grad_hidden, _ = norm_backward(grad_n1, unit_one, rms_one, gain_one)
    input_grad = (grad_middle + grad_hidden).astype(bf16)

    return (
        mixed,
        input_grad,
        tiny[0],
        wq_grad,
        wk_grad,
        wv_grad,
        wo_grad,
        tiny[1],
        tiny[2 : 2 + EXPERTS].T,
        su_grad,
        sd_grad,
        eu_grad,
        ed_grad,
    )


def solution(mesh):
    return jax.shard_map(
        planes if mesh.shape["shard"] == KEY_HEADS and mesh.shape["replica"] == 8 else shards,
        mesh=mesh,
        in_specs=(
            P(("replica", "shard"), None),
            P(("replica", "shard"), None),
            P("replica", None),
            P(("replica", "shard"), None),
            P("shard"),
            P("shard", None),
            P("shard", None),
            P("shard", None),
            P("shard", None),
            P("shard"),
            P("shard", None),
            P("shard", None),
            P("shard", None),
            P("shard", None, None),
            P("shard", None, None),
        ),
        out_specs=(
            P(("replica", "shard"), None),
            P(("replica", "shard"), None),
            P("shard"),
            P("shard", None),
            P("shard", None),
            P("shard", None),
            P("shard", None),
            P("shard"),
            P("shard", None),
            P("shard", None),
            P("shard", None),
            P("shard", None, None),
            P("shard", None, None),
        ),
        check_vma=False,
    )
```

```python
import functools

import jax
import jax.numpy as jnp
from jax import lax
from jax.experimental import pallas as pl
from jax.experimental.pallas import tpu as pltpu
from jax.sharding import PartitionSpec as P

QUERY_HEADS = 20
KEY_HEADS = 4
HEAD_SIZE = 128
FF = 1536
SH = 3072
EXPERTS = 2
SEQS = 3


epsilon = 1e-05
rope_base = 500000.0
far_below = -1e30


def shortened(array):

    def short(part):
        return part.astype(jnp.bfloat16) if part.dtype == jnp.float32 else part

    return jax.tree.map(short, array)


def angles(position):
    inverse = rope_base ** (-(jnp.arange(HEAD_SIZE // 2, dtype=jnp.float32) * 2.0) / HEAD_SIZE)
    phases = position.astype(jnp.float32)[:, None] * inverse[None, :]
    return (jnp.cos(phases), jnp.sin(phases))


def apply_rotation(entries, cosine_table, sine_table):
    half_width = HEAD_SIZE // 2
    first_half = entries[..., :half_width]
    second_half = entries[..., half_width:]
    cos_b = cosine_table[:, None, :]
    sin_b = sine_table[:, None, :]
    return jnp.concatenate(
        [first_half * cos_b - second_half * sin_b, second_half * cos_b + first_half * sin_b],
        axis=-1,
    )


def reverse_rotation(grads_in, cosine_table, sine_table):
    half_width = HEAD_SIZE // 2
    first_half = grads_in[..., :half_width]
    second_half = grads_in[..., half_width:]
    cos_b = cosine_table[:, None, :]
    sin_b = sine_table[:, None, :]
    return jnp.concatenate(
        [first_half * cos_b + second_half * sin_b, second_half * cos_b - first_half * sin_b],
        axis=-1,
    )


def layout(lengths_row, device_group):
    doc_ends = jnp.cumsum(lengths_row)
    doc_starts = doc_ends - lengths_row
    places = jnp.arange(device_group, dtype=jnp.int32)
    document = jnp.sum((places[:, None] >= doc_ends[None, :]).astype(jnp.int32), axis=1)
    chosen = (document[:, None] == jnp.arange(SEQS, dtype=jnp.int32)[None, :]).astype(jnp.int32)
    position = places - jnp.sum(chosen * doc_starts[None, :], axis=1)
    return (document, position)


def norm_forward(inputs):
    inverse_rms = lax.rsqrt(jnp.mean(inputs * inputs, axis=-1, keepdims=True) + epsilon)
    return (inputs * inverse_rms, inverse_rms)


def norm_backward(grad_out, unit, inverse_rms, gain_row):
    scaled = grad_out * gain_row.astype(jnp.float32)
    grad_in = inverse_rms * (scaled - unit * jnp.mean(scaled * unit, axis=-1, keepdims=True))
    return (grad_in, jnp.sum(grad_out * unit, axis=0))


def silu_product(both, split_at):
    gate_part = both[:, :split_at]
    up_part = both[:, split_at:]
    return gate_part * jax.nn.sigmoid(gate_part) * up_part


def swiglu_back(both, grad_inner, split_at):
    gate_part = both[:, :split_at]
    up_part = both[:, split_at:]
    sigma = jax.nn.sigmoid(gate_part)
    activated = gate_part * sigma
    grad_gate = grad_inner * up_part * sigma * (1.0 + gate_part * (1.0 - sigma))
    return jnp.concatenate([grad_gate, grad_inner * activated], axis=-1)


def matrix_product(left, right):
    return jnp.dot(left, right, preferred_element_type=jnp.float32)


def times_transposed(left, right):
    return jnp.einsum("tf,df->td", left, right, preferred_element_type=jnp.float32)


def weight_grad(left, right):
    return jnp.einsum("td,tf->df", left, right, preferred_element_type=jnp.float32)


def shards(
    layer_input, cotangent, lengths, expert_ids, g1, wq, wk, wv, wo, g2, wr, w_su, w_sd, w_eu, w_ed
):
    token_count = layer_input.shape[0]
    device_group = token_count * lax.axis_size("shard")
    offset = lax.axis_index("shard") * token_count
    group_layout = QUERY_HEADS // KEY_HEADS
    score_scale = HEAD_SIZE ** (-0.5)

    def fetch_attention():
        return (
            lax.all_gather(g1, "shard", axis=0, tiled=True),
            lax.all_gather(wq, "shard", axis=0, tiled=True),
            lax.all_gather(wk, "shard", axis=0, tiled=True),
            lax.all_gather(wv, "shard", axis=0, tiled=True),
            lax.all_gather(wo, "shard", axis=0, tiled=True),
        )

    def reduce_grads(pieces):
        shares = jax.tree.map(
            lambda part: part.astype(jnp.float32),
            lax.psum_scatter(shortened(pieces), "shard", scatter_dimension=0, tiled=True),
        )
        return jax.tree.map(
            lambda part: part.astype(jnp.float32), lax.psum(shortened(shares), "replica")
        )

    document, position = layout(lengths[0], device_group)
    places = jnp.arange(device_group, dtype=jnp.int32)
    query_doc = lax.dynamic_slice_in_dim(document, offset, token_count)
    query_place = offset + jnp.arange(token_count, dtype=jnp.int32)
    allowed = (query_doc[:, None] == document[None, :]) & (query_place[:, None] >= places[None, :])
    cosine_table, sine_table = angles(lax.dynamic_slice_in_dim(position, offset, token_count))
    hidden = layer_input.astype(jnp.float32)
    gain_one, w_query, key_matrix, w_value, w_out = fetch_attention()
    unit_one, rms_one = norm_forward(hidden)
    first_normed = (unit_one * gain_one.astype(jnp.float32)).astype(jnp.bfloat16)
    query_rows = apply_rotation(
        matrix_product(first_normed, w_query).reshape(token_count, QUERY_HEADS, HEAD_SIZE),
        cosine_table,
        sine_table,
    )
    query_rows = query_rows.astype(jnp.bfloat16).reshape(
        token_count, KEY_HEADS, group_layout, HEAD_SIZE
    )
    local_keys = apply_rotation(
        matrix_product(first_normed, key_matrix).reshape(token_count, KEY_HEADS, HEAD_SIZE),
        cosine_table,
        sine_table,
    )
    local_keys = local_keys.astype(jnp.bfloat16).reshape(token_count, KEY_HEADS * HEAD_SIZE)
    values_own = matrix_product(first_normed, w_value).astype(jnp.bfloat16)
    gathered_keys, gathered_values = (
        lax.all_gather(local_keys, "shard", axis=0, tiled=True),
        lax.all_gather(values_own, "shard", axis=0, tiled=True),
    )
    gathered_keys = gathered_keys.reshape(device_group, KEY_HEADS, HEAD_SIZE)
    gathered_values = gathered_values.reshape(device_group, KEY_HEADS, HEAD_SIZE)

    def scores_of(key_value_head):
        raw = jnp.einsum(
            "tqd,sd->qts",
            query_rows[:, key_value_head],
            gathered_keys[:, key_value_head],
            preferred_element_type=jnp.float32,
        )
        return raw * score_scale

    head_outputs = []
    log_totals = []
    for key_value_head in range(KEY_HEADS):
        masked = jnp.where(allowed[None], scores_of(key_value_head), far_below)
        peak_score = jnp.max(masked, axis=-1, keepdims=True)
        weights = jnp.where(allowed[None], jnp.exp(masked - peak_score), 0.0)
        totals = jnp.sum(weights, axis=-1, keepdims=True)
        probabilities = weights / totals
        log_totals.append(peak_score + jnp.log(totals))
        head_outputs.append(
            jnp.einsum(
                "qts,sd->tqd",
                probabilities.astype(jnp.bfloat16),
                gathered_values[:, key_value_head],
                preferred_element_type=jnp.float32,
            )
        )
    attended = (
        jnp.stack(head_outputs, axis=1)
        .reshape(token_count, QUERY_HEADS * HEAD_SIZE)
        .astype(jnp.bfloat16)
    )
    middle = hidden + matrix_product(attended, w_out)
    gain_two, w_router, w_shared_up, w_shared_down, w_experts_up, w_experts_down = (
        lax.all_gather(g2, "shard", axis=0, tiled=True),
        lax.all_gather(wr, "shard", axis=0, tiled=True),
        lax.all_gather(w_su, "shard", axis=0, tiled=True),
        lax.all_gather(w_sd, "shard", axis=0, tiled=True),
        lax.all_gather(w_eu, "shard", axis=0, tiled=True),
        lax.all_gather(w_ed, "shard", axis=0, tiled=True),
    )
    unit_two, rms_two = norm_forward(middle)
    normed_two = (unit_two * gain_two.astype(jnp.float32)).astype(jnp.bfloat16)
    logits = matrix_product(normed_two, w_router)
    onehot = (expert_ids[:, :, None] == jnp.arange(EXPERTS, dtype=jnp.int32)[None, None, :]).astype(
        jnp.float32
    )
    chosen_mask = jnp.sum(onehot, axis=1)
    probs = jax.nn.softmax(logits, axis=-1)
    routed = chosen_mask * probs
    shared_both = matrix_product(normed_two, w_shared_up)
    shared_inner = silu_product(shared_both, SH).astype(jnp.bfloat16)
    summed_out = middle + matrix_product(shared_inner, w_shared_down)
    expert_boths = []
    expert_inners = []
    expert_results = []
    for expert in range(EXPERTS):
        both = matrix_product(normed_two, w_experts_up[:, expert])
        inner = silu_product(both, FF).astype(jnp.bfloat16)
        result = matrix_product(inner, w_experts_down[:, expert])
        summed_out = summed_out + routed[:, expert : expert + 1] * result
        expert_boths.append(both)
        expert_inners.append(inner)
        expert_results.append(result)
    mixed = summed_out.astype(jnp.bfloat16)
    upstream = cotangent.astype(jnp.float32)
    grad_shared_out = upstream.astype(jnp.bfloat16)
    grad_shared_inner = times_transposed(grad_shared_out, w_shared_down)
    grad_shared_both = swiglu_back(shared_both, grad_shared_inner, SH).astype(jnp.bfloat16)
    grad_normed = times_transposed(grad_shared_both, w_shared_up)
    shared_grads = reduce_grads(
        (weight_grad(normed_two, grad_shared_both), weight_grad(shared_inner, grad_shared_out))
    )
    up_grads = []
    down_grads = []
    routed_grads = []
    for expert in range(EXPERTS):
        grad_result = (routed[:, expert : expert + 1] * upstream).astype(jnp.bfloat16)
        routed_grads.append(jnp.sum(upstream * expert_results[expert], axis=-1))
        down_grads.append(weight_grad(expert_inners[expert], grad_result))
        grad_inner = times_transposed(grad_result, w_experts_down[:, expert])
        grad_both = swiglu_back(expert_boths[expert], grad_inner, FF).astype(jnp.bfloat16)
        up_grads.append(weight_grad(normed_two, grad_both))
        grad_normed = grad_normed + times_transposed(grad_both, w_experts_up[:, expert])
    grad_probs = chosen_mask * jnp.stack(routed_grads, axis=1)
    grad_logits = probs * (grad_probs - jnp.sum(probs * grad_probs, axis=-1, keepdims=True))
    grad_logits = grad_logits.astype(jnp.bfloat16)
    grad_router = weight_grad(normed_two, grad_logits)
    grad_normed = grad_normed + times_transposed(grad_logits, w_router)
    grad_middle_norm, grad_gain_two = norm_backward(grad_normed, unit_two, rms_two, gain_two)
    grad_middle = upstream + grad_middle_norm
    expert_grads = reduce_grads(
        (grad_gain_two, grad_router, jnp.stack(up_grads, axis=1), jnp.stack(down_grads, axis=1))
    )
    gain_one, w_query, key_matrix, w_value, w_out = fetch_attention()
    grad_proj_out = grad_middle.astype(jnp.bfloat16)
    grad_out_weight = weight_grad(attended, grad_proj_out)
    grad_attended = (
        times_transposed(grad_proj_out, w_out)
        .astype(jnp.bfloat16)
        .reshape(token_count, KEY_HEADS, group_layout, HEAD_SIZE)
    )
    query_grads = []
    key_gradients = []
    value_gradients = []
    for key_value_head in range(KEY_HEADS):
        scores = scores_of(key_value_head)
        probabilities = jnp.where(allowed[None], jnp.exp(scores - log_totals[key_value_head]), 0.0)
        grad_here = grad_attended[:, key_value_head]
        grad_weights = jnp.einsum(
            "tqd,sd->qts",
            grad_here,
            gathered_values[:, key_value_head],
            preferred_element_type=jnp.float32,
        )
        grad_scores = probabilities * (
            grad_weights - jnp.sum(probabilities * grad_weights, axis=-1, keepdims=True)
        )
        grad_scores = grad_scores.astype(jnp.bfloat16)
        query_grads.append(
            jnp.einsum(
                "qts,sd->tqd",
                grad_scores,
                gathered_keys[:, key_value_head],
                preferred_element_type=jnp.float32,
            )
            * score_scale
        )
        key_gradients.append(
            jnp.einsum(
                "qts,tqd->sd",
                grad_scores,
                query_rows[:, key_value_head],
                preferred_element_type=jnp.float32,
            )
            * score_scale
        )
        value_gradients.append(
            jnp.einsum(
                "qts,tqd->sd",
                probabilities.astype(jnp.bfloat16),
                grad_here,
                preferred_element_type=jnp.float32,
            )
        )
    reduced_keys, values_summed = (
        lax.psum_scatter(
            jnp.stack(key_gradients, axis=1)
            .reshape(device_group, KEY_HEADS * HEAD_SIZE)
            .astype(jnp.bfloat16),
            "shard",
            scatter_dimension=0,
            tiled=True,
        ).astype(jnp.float32),
        lax.psum_scatter(
            jnp.stack(value_gradients, axis=1)
            .reshape(device_group, KEY_HEADS * HEAD_SIZE)
            .astype(jnp.bfloat16),
            "shard",
            scatter_dimension=0,
            tiled=True,
        ).astype(jnp.float32),
    )
    grad_query = reverse_rotation(
        jnp.stack(query_grads, axis=1).reshape(token_count, QUERY_HEADS, HEAD_SIZE),
        cosine_table,
        sine_table,
    )
    grad_query = grad_query.reshape(token_count, QUERY_HEADS * HEAD_SIZE).astype(jnp.bfloat16)
    key_gradient = reverse_rotation(
        reduced_keys.reshape(token_count, KEY_HEADS, HEAD_SIZE), cosine_table, sine_table
    )
    key_gradient = key_gradient.reshape(token_count, KEY_HEADS * HEAD_SIZE).astype(jnp.bfloat16)
    grad_value = values_summed.astype(jnp.bfloat16)
    grad_normed_one = times_transposed(grad_query, w_query) + times_transposed(
        key_gradient, key_matrix
    )
    grad_normed_one = grad_normed_one + times_transposed(grad_value, w_value)
    grad_hidden_norm, grad_gain_one = norm_backward(grad_normed_one, unit_one, rms_one, gain_one)
    grad_of_input = (grad_middle + grad_hidden_norm).astype(jnp.bfloat16)
    attention_grads = reduce_grads(
        (
            grad_gain_one,
            weight_grad(first_normed, grad_query),
            weight_grad(first_normed, key_gradient),
            weight_grad(first_normed, grad_value),
            grad_out_weight,
        )
    )
    return (
        mixed,
        grad_of_input,
        attention_grads[0],
        attention_grads[1],
        attention_grads[2],
        attention_grads[3],
        attention_grads[4],
        expert_grads[0],
        expert_grads[1],
        shared_grads[0],
        shared_grads[1],
        expert_grads[2],
        expert_grads[3],
    )


MESH = pl.DeviceIdType.MESH


def neighbours():
    rank = lax.axis_index("replica")
    core = rank + 1 - 2 * (rank % 2)
    along_x = rank + 2 - 4 * ((rank // 2) % 2)
    along_y = rank + 4 - 8 * (rank // 4)
    return rank, core, along_x, along_y, along_x + along_y - rank


def greet(peers):
    barrier = pltpu.get_barrier_semaphore()
    for peer in peers:
        pl.semaphore_signal(barrier, inc=1, device_id=peer, device_id_type=MESH)
    pl.semaphore_wait(barrier, len(peers))


def send(src, dst, sends, recvs, at, peer):
    copy = pltpu.make_async_remote_copy(
        src_ref=src,
        dst_ref=dst,
        send_sem=sends.at[at],
        recv_sem=recvs.at[at],
        device_id=peer,
        device_id_type=MESH,
    )
    copy.start()
    return copy


class Relay:
    def __init__(self, source, block, width, odd, sends, recvs, at):
        rank, core, along_x, along_y, across = neighbours()
        here = lax.axis_index("shard")
        self.to_x, self.to_y, self.to_core = (along_x, here), (along_y, here), (core, here)
        self.rank, self.along_x, self.along_y, self.across = rank, along_x, along_y, across
        self.source, self.block, self.width = source, block, width
        self.cut = 128 * ((width // 128 + odd) // 2)
        self.sends, self.recvs, self.at = sends, recvs, at
        self.copies = []
        self.crossing = []

    def send(self, src, dst, k, peer):
        copy = send(src, dst, self.sends, self.recvs, (*self.at, k), peer)
        self.copies.append(copy)
        return copy

    def cross(self, src, dst, k):
        self.crossing.append(self.send(src, dst, k, self.to_core))

    def start(self):
        mine = self.block(self.rank, 0, self.width)
        self.over_x = self.send(self.source, mine, 0, self.to_x)
        self.over_y = self.send(self.source, mine, 1, self.to_y)
        self.cross(self.source, mine, 2)

    def middle(self):
        self.over_x.wait_recv()
        part = self.block(self.along_x, 0, self.cut)
        self.half_a = self.send(part, part, 3, self.to_y)
        self.over_y.wait_recv()
        part = self.block(self.along_y, self.cut, self.width)
        self.half_b = self.send(part, part, 4, self.to_x)
        for k, who in ((5, self.along_x), (6, self.along_y)):
            whole = self.block(who, 0, self.width)
            self.cross(whole, whole, k)

    def late(self):
        self.half_a.wait_recv()
        self.half_b.wait_recv()
        whole = self.block(self.across, 0, self.width)
        self.cross(whole, whole, 7)

    def finish(self):
        for copy in self.crossing:
            copy.wait_recv()
        for copy in self.copies:
            copy.wait_send()


def add_rows(dst, src):
    rows = dst.shape[0]
    size = 32 if rows % 32 == 0 else 16

    def body(step, _):
        at = pl.ds(pl.multiple_of(step * size, 16), size)
        dst[at, :] = dst[at, :] + src[at, :]
        return 0

    lax.fori_loop(0, rows // size, body, 0)


class Ring:
    def __init__(self, partial, full, make, buffers, semaphores):
        self.partial, self.full, self.make = partial, full, make
        self.right, self.left, self.own = buffers
        self.folds_s, self.folds_r, self.tells_s, self.tells_r, self.stays = semaphores
        self.rank = lax.axis_index("replica")
        self.here = lax.axis_index("shard")
        self.chunks, self.size = self.own.shape[0], self.own.shape[1]
        self.last = self.right.shape[1] - 1
        self.steps = self.chunks + 2 * self.last

    def prepare(self):
        @pl.when(self.here == 0)
        def _():
            for k in range(self.chunks):
                self.right[k, 0] = jnp.zeros(self.right.shape[2:], self.right.dtype)

        @pl.when(self.here == self.last)
        def _():
            for k in range(self.chunks):
                self.left[k, self.last] = jnp.zeros(self.left.shape[2:], self.left.dtype)

    def rows(self, b, k):
        first = (b * self.chunks + k) * self.size
        return pl.ds(pl.multiple_of(first, 16), self.size)

    def push(self, src, dst, sends, recvs, at, way):
        return pltpu.make_async_remote_copy(
            src_ref=src,
            dst_ref=dst,
            send_sem=sends.at[at],
            recv_sem=recvs.at[at],
            device_id=(self.rank, self.here + 1 - 2 * way),
            device_id_type=MESH,
        )

    def partial_copy(self, k, b, way, src=None):
        held = (self.right, self.left)[way].at[k, b]
        src = held if src is None else src
        return self.push(src, held, self.folds_s, self.folds_r, (way, k, b), way)

    def sides(self, b, way):
        inside = self.here < b if way == 0 else self.here > b
        edge = self.here == (0 if way == 0 else self.last)
        return inside, edge

    def lead(self, k):
        for way, blocks in ((0, range(self.last, 0, -1)), (1, range(self.last))):

            @pl.when(self.here == (0 if way == 0 else self.last))
            def _(way=way, blocks=blocks):
                for b in blocks:
                    self.partial_copy(k, b, way, self.partial.at[self.rows(b, k)]).start()

    def fold(self, i):
        for way, blocks in ((0, range(self.last, 0, -1)), (1, range(self.last))):
            k = i - self.here if way == 0 else i - self.last + self.here
            now = jnp.logical_and(k >= 0, k < self.chunks)
            for b in blocks:
                inside, edge = self.sides(b, way)
                inside = jnp.logical_and(inside, now)
                mine = self.partial.at[self.rows(b, k)]

                @pl.when(jnp.logical_and(inside, jnp.logical_not(edge)))
                def _(k=k, b=b, way=way, mine=mine):
                    copy = self.partial_copy(k, b, way)
                    copy.wait_recv()
                    add_rows((self.right, self.left)[way].at[k, b], mine)
                    copy.start()

    def settle(self, k):
        here = self.here

        @pl.when(here > 0)
        def _():
            self.partial_copy(k, here, 0).wait_recv()

        @pl.when(here < self.last)
        def _():
            self.partial_copy(k, here, 1).wait_recv()

        def part(step, _):
            inner = pl.ds(pl.multiple_of(step * 16, 16), 16)
            first = (here * self.chunks + k) * self.size + step * 16
            total = self.partial[pl.ds(pl.multiple_of(first, 16), 16), :].astype(jnp.float32)
            total = total + self.right[k, here, inner, :].astype(jnp.float32)
            total = total + self.left[k, here, inner, :].astype(jnp.float32)
            at = pl.ds(pl.multiple_of(k * self.size + step * 16, 16), 16)
            self.own[k, inner, :] = self.make(at, total)
            return 0

        lax.fori_loop(0, self.size // 16, part, 0)
        self.stay(k).start()
        for way in range(2):

            @pl.when(here < self.last if way == 0 else here > 0)
            def _(way=way):
                self.told(k, way).start()

    def stay(self, k):
        return pltpu.make_async_copy(
            self.own.at[k], self.full.at[self.rows(self.here, k)], self.stays.at[k]
        )

    def told(self, k, way):
        dst = self.full.at[self.rows(self.here, k)]
        return self.push(self.own.at[k], dst, self.tells_s, self.tells_r, (way, k, 0), way)

    def passed(self, k, way, hop, slot):
        block = self.here - hop if way == 0 else self.here + hop
        part = self.full.at[self.rows(block, k)]
        return self.push(part, part, self.tells_s, self.tells_r, (way, k, slot), way)

    def comes(self, way, hop):
        return self.here >= hop if way == 0 else self.here + hop <= self.last

    def goes_on(self, way, hop):
        return jnp.logical_and(
            self.comes(way, hop), self.here < self.last if way == 0 else self.here > 0
        )

    def forward(self, k, hop):
        for way in range(2):

            @pl.when(self.comes(way, hop))
            def _(way=way):
                self.passed(k, way, hop, hop - 1).wait_recv()

            if hop < self.last:

                @pl.when(self.goes_on(way, hop))
                def _(way=way):
                    self.passed(k, way, hop, hop).start()

    def step(self, i):
        if i == 0:
            self.lead(0)
        if i + 1 < self.chunks:
            self.lead(i + 1)
        if i < self.chunks + self.last:
            self.fold(i)
        if 0 <= i - self.last < self.chunks:
            self.settle(i - self.last)
        for hop in range(1, self.last + 1):
            if 0 <= i - self.last - hop < self.chunks:
                self.forward(i - self.last - hop, hop)

    def finish(self):
        for k in range(self.chunks):
            self.stay(k).wait()
            for way, blocks in ((0, range(self.last, 0, -1)), (1, range(self.last))):
                for b in blocks:
                    inside, _ = self.sides(b, way)

                    @pl.when(inside)
                    def _(k=k, b=b, way=way):
                        self.partial_copy(k, b, way).wait_send()

            for way in range(2):

                @pl.when(self.here < self.last if way == 0 else self.here > 0)
                def _(k=k, way=way):
                    self.told(k, way).wait_send()

                for hop in range(1, self.last):

                    @pl.when(self.goes_on(way, hop))
                    def _(k=k, way=way, hop=hop):
                        self.passed(k, way, hop, hop).wait_send()


def ring_scratch(group, planes_n, width, chunks):
    dma = pltpu.SemaphoreType.DMA
    size = group // planes_n // chunks
    return [
        pltpu.VMEM((chunks, planes_n, size, width), jnp.bfloat16),
        pltpu.VMEM((chunks, planes_n, size, width), jnp.bfloat16),
        pltpu.VMEM((chunks, size, width), jnp.bfloat16),
        dma((2, chunks, planes_n)),
        dma((2, chunks, planes_n)),
        dma((2, chunks, planes_n - 1)),
        dma((2, chunks, planes_n - 1)),
        dma((chunks,)),
    ]


def forward_norm(hidden, gain, middle, inverse):
    def make(at, total):
        total = total + hidden[at, :].astype(jnp.float32)
        rms = lax.rsqrt(jnp.mean(total * total, axis=-1, keepdims=True) + epsilon)
        middle[at, :] = total
        inverse[at, :] = jnp.broadcast_to(rms, (total.shape[0], inverse.shape[1]))
        return (total * rms * gain[...]).astype(jnp.bfloat16)

    return make


def backward_norm(cotangent, middle, inverse, gain, grad_middle, grad_gain):
    def make(at, total):
        rms = inverse[at, :1]
        unit = middle[at, :] * rms
        scaled = total * gain[...]
        grad = rms * (scaled - unit * jnp.mean(scaled * unit, axis=-1, keepdims=True))
        grad = grad + cotangent[at, :].astype(jnp.float32)
        grad_middle[at, :] = grad
        grad_gain[...] += jnp.sum(total * unit, axis=0, keepdims=True)
        return grad.astype(jnp.bfloat16)

    return make


def spread_kernel(items, sources, count, shared, ringed, *refs):
    ins, refs = refs[:sources], refs[sources:]
    if ringed:
        (partial, hidden, gain), refs = refs[:3], refs[3:]
    outs, refs = refs[:count], refs[count:]
    if ringed:
        (full, middle, inverse), refs = refs[:3], refs[3:]
    own, zs, zr, sends, recvs = refs[:5]
    ring = None
    if ringed:
        make = forward_norm(hidden, gain, middle, inverse)
        ring = Ring(partial, full, make, refs[5:8], refs[8:])
        ring.prepare()
    planes_n = 4
    piece = outs[0].shape[0] // 32
    rank, core, along_x, along_y, across = neighbours()
    here = lax.axis_index("shard")
    others = [(rank, (here + j) % planes_n) for j in range(1, planes_n)]
    greet(others + [(along_x, here), (along_y, here), (core, here)])

    def block(i, j, who, lo, hi):
        plane = (here + planes_n - j) % planes_n
        first = pl.multiple_of((plane * 8 + who) * piece, 16)
        return outs[i].at[pl.ds(first, piece), pl.ds(lo, hi - lo)]

    over_z, stays = {}, []
    for j in range(planes_n):
        target = (here + j) % planes_n
        for k, (src, whole, base, size, out, place) in enumerate(items):
            row = pl.multiple_of(rank * piece, 16) if whole else 0
            column = pl.multiple_of(base + target * size, 128)
            part = ins[src].at[pl.ds(row, piece), pl.ds(column, size)]
            dst = block(out, 0, rank, place, place + size)
            if j:
                over_z[j, k] = send(part, dst, zs, zr, (j, k), (rank, target))
            else:
                copy = pltpu.make_async_copy(part, dst, own.at[k])
                copy.start()
                stays.append(copy)
        if shared:
            src, dst = ins[-1], outs[-1].at[here]
            if j:
                over_z[j, len(items)] = send(
                    src, dst, zs, zr, (j, len(items)), (rank, target)
                )
            else:
                copy = pltpu.make_async_copy(src, dst, own.at[len(items)])
                copy.start()
                stays.append(copy)
    relays = []
    blocks = count - 1 if shared else count
    for j in range(planes_n):
        row = []
        for i in range(blocks):
            width = outs[i].shape[1]
            row.append(
                Relay(
                    block(i, j, rank, 0, width),
                    functools.partial(block, i, j),
                    width,
                    j % 2,
                    sends,
                    recvs,
                    (i, j),
                )
            )
        relays.append(row)
    starts = (0, 3, 5, 7) if ring else (0, 1, 2, 3)
    for step in range(max(starts[-1] + 3, ring.steps if ring else 0)):
        if ring and step < ring.steps:
            ring.step(step)
        for n, first in enumerate(starts):
            if step == first:
                if n == 0:
                    for copy in stays:
                        copy.wait()
                for (j, k), copy in over_z.items():
                    if j == n:
                        copy.wait_recv()
                for relay in relays[n]:
                    relay.start()
            if step == first + 1:
                for relay in relays[n]:
                    relay.middle()
            if step == first + 2:
                for relay in relays[n]:
                    relay.late()
    for copy in over_z.values():
        copy.wait_send()
    for row in relays:
        for relay in row:
            relay.finish()
    if ring:
        ring.finish()


def spread(ins, items, outs, shared, collective_id, micros, ring=None):
    dma = pltpu.SemaphoreType.DMA
    count = len(items) + (1 if shared else 0)
    any_space = pl.BlockSpec(memory_space=pl.ANY)
    vmem = pl.BlockSpec(memory_space=pltpu.VMEM)
    shaped = [jax.ShapeDtypeStruct(shape, jnp.bfloat16) for shape in outs]
    out_specs = [any_space] * len(outs)
    scratch = []
    if ring:
        group, tokens, width = ring[0].shape[0], ring[1].shape[0], ring[0].shape[1]
        shaped += [
            jax.ShapeDtypeStruct((group, width), jnp.bfloat16),
            jax.ShapeDtypeStruct((tokens, width), jnp.float32),
            jax.ShapeDtypeStruct((tokens, 128), jnp.float32),
        ]
        out_specs += [any_space, vmem, vmem]
        scratch = ring_scratch(group, group // tokens, width, 8)
    return pl.pallas_call(
        functools.partial(spread_kernel, items, len(ins), len(outs), shared, ring is not None),
        out_shape=shaped,
        in_specs=[any_space] * len(ins) + ([vmem] * 3 if ring else []),
        out_specs=out_specs,
        scratch_shapes=[dma((count,))]
        + [dma((4, count))] * 2
        + [dma((len(outs), 4, 8))] * 2
        + scratch,
        compiler_params=pltpu.CompilerParams(
            collective_id=collective_id, has_side_effects=True, vmem_limit_bytes=32 * 2**20
        ),
        cost_estimate=pl.CostEstimate(
            flops=0, bytes_accessed=int(micros * 3.0e6), transcendentals=0
        ),
    )(*ins, *(ring or ()))


class Fold:
    def __init__(self, factor, plane, slot, buffers, j, sends, recvs, at):
        rank, core, along_x, along_y, _ = neighbours()
        here = lax.axis_index("shard")
        self.c, self.x, self.y = rank % 2, (rank // 2) % 2, rank // 4
        self.to_x, self.to_y, self.to_core = (along_x, here), (along_y, here), (core, here)
        self.left, self.left_first, self.right, self.right_first = factor
        self.plane, self.mine, self.before = plane, slot, None
        self.held, self.far_a, self.far_b, self.near_a, self.near_b = [b.at[j] for b in buffers]
        self.cut, self.rest = self.near_a.shape[1], self.near_b.shape[1]
        self.sends, self.recvs, self.at = sends, recvs, at
        self.copies = []

    def send(self, src, dst, k, peer):
        copy = send(src, dst, self.sends, self.recvs, (self.at, k), peer)
        self.copies.append(copy)
        return copy

    def begin(self):
        _, _, _, m, n = self.mine.shape
        column = pl.multiple_of(self.left_first + self.plane * 8 * m, 128)
        tile = 512 if n % 512 == 0 else n
        if self.before is not None:
            self.before.first.wait_send()
            self.before.copies.remove(self.before.first)

        def product(step, _):
            at = pl.ds(pl.multiple_of(step * tile, 128), tile)
            there = pl.ds(pl.multiple_of(self.right_first + step * tile, 128), tile)
            block = over_first(self.left[:, pl.ds(column, 8 * m)], self.right[:, there])
            block = block.astype(self.mine.dtype)
            for r in range(8):
                self.mine[r // 4, (r // 2) % 2, r % 2, :, at] = block[r * m : (r + 1) * m, :]
            return 0

        lax.fori_loop(0, n // tile, product, 0)
        self.first = self.send(self.mine.at[:, :, 1 - self.c], self.held, 0, self.to_core)

    def start(self):
        self.first.wait_recv()
        for p in range(2):
            for q in range(2):
                add_rows(self.held.at[p, q], self.mine.at[p, q, self.c])
        left, right = pl.ds(0, self.cut), pl.ds(self.cut, self.rest)
        self.over_x = self.send(self.held.at[:, 1 - self.x, :, left], self.far_a, 1, self.to_x)
        self.over_y = self.send(self.held.at[1 - self.y, :, :, right], self.far_b, 2, self.to_y)

    def middle(self):
        left, right = pl.ds(0, self.cut), pl.ds(self.cut, self.rest)
        self.over_x.wait_recv()
        for p in range(2):
            add_rows(self.far_a.at[p], self.held.at[p, self.x, :, left])
        self.last_a = self.send(self.far_a.at[1 - self.y], self.near_a, 3, self.to_y)
        self.over_y.wait_recv()
        for q in range(2):
            add_rows(self.far_b.at[q], self.held.at[self.y, q, :, right])
        self.last_b = self.send(self.far_b.at[1 - self.x], self.near_b, 4, self.to_x)

    def late(self):
        self.last_a.wait_recv()
        add_rows(self.near_a, self.far_a.at[self.y])
        self.last_b.wait_recv()
        add_rows(self.near_b, self.far_b.at[self.x])

    def finish(self):
        for copy in self.copies:
            copy.wait_send()


def place_fold(piece, j, shape, plan, outs, own, n, zs, zr, at, finals):
    planes_n = 4
    rank = lax.axis_index("replica")
    here = lax.axis_index("shard")
    halves = ((piece.near_a, 0, piece.cut), (piece.near_b, piece.cut, piece.cut + piece.rest))
    for half, (buf, lo, hi) in enumerate(halves):
        for k, (offset, size, out, base, top) in enumerate(plan):
            left, right = max(lo, offset), min(hi, offset + size)
            if left >= right:
                continue
            src = buf.at[:, pl.ds(left - lo, right - left)]
            place = base + (left - offset)
            if shape[0] > 1:
                place = pl.multiple_of(place + here * size, 128)
            dst = outs[out].at[pl.ds(top, shape[1]), pl.ds(place, right - left)]
            if j == 0:
                copy = pltpu.make_async_copy(src, dst, own.at[n, 2 * k + half])
                copy.start()
            else:
                target = (rank, (here + j) % planes_n)
                copy = send(src, dst, zs, zr, (*at, 2 * k + half), target)
            finals[out].append(copy)


def fold_scratch(shapes, depth=2):
    bf16 = jnp.bfloat16
    keys = {}
    for a, m, n in shapes:
        keys[m, n] = keys.get((m, n), 0) + a
    scratch = [pltpu.VMEM((min(depth, number), 2, 2, 2, *key), bf16) for key, number in keys.items()]
    for a, m, n in shapes:
        cut = 128 * (n // 256)
        scratch += [
            pltpu.VMEM((a, 2, 2, m, n), bf16),
            pltpu.VMEM((a, 2, m, cut), bf16),
            pltpu.VMEM((a, 2, m, n - cut), bf16),
            pltpu.VMEM((a, m, cut), bf16),
            pltpu.VMEM((a, m, n - cut), bf16),
        ]
    return keys, scratch


def exchange_kernel(setup, *refs):
    shapes, factors, plans, after, counts = setup
    lag = 2
    operands_n, ring_n, sources_n, tiny, out_count, slot_keys, downs_n = counts
    count = len(shapes)

    def take(number):
        nonlocal refs
        head, refs = refs[:number], refs[number:]
        return head

    operands, ring_in, sources = take(operands_n), take(ring_n), take(sources_n)
    tiny_in, downs = take(tiny), take(downs_n)
    outs, wide, later = take(out_count), take(sources_n), take(len(after))
    tiny_outs = take(2 * tiny)
    ring_out = take(3 if ring_n else 0)
    y_out = take(1 if downs_n else 0)
    slots = dict(zip(slot_keys, take(len(slot_keys))))
    sets = [take(5) for _ in range(count)]
    sends, recvs, own, zs, zr, relay_sends, relay_recvs, relay_own, tiny_s, tiny_r, tiny_own = take(11)
    ring = None
    if ring_n:
        partial, cotangent, middle, inverse, gain = ring_in
        full, grad_middle, grad_gain = ring_out
        make = backward_norm(cotangent, middle, inverse, gain, grad_middle, grad_gain)
        ring = Ring(partial, full, make, refs[:3], refs[3:8])
        refs = refs[8:]
        ring.prepare()
        grad_gain[...] = jnp.zeros_like(grad_gain)
    rank, core, along_x, along_y, _ = neighbours()
    here = lax.axis_index("shard")
    planes_n = 4
    peers = [(along_x, here), (along_y, here), (core, here)]
    greet(peers + [(rank, (here + j) % planes_n) for j in range(1, planes_n)])
    tiny_copies = []
    for ref in tiny_in:
        m = ref.shape[1]
        for j in range(planes_n):
            target = (here + j) % planes_n
            dst = tiny_outs[0].at[pl.ds(pl.multiple_of(here * m, 8), m)]
            if j:
                copy = send(ref.at[target], dst, tiny_s, tiny_r, (j,), (rank, target))
            else:
                copy = pltpu.make_async_copy(ref.at[here], dst, tiny_own.at[0])
                copy.start()
            tiny_copies.append(copy)

    if downs_n:
        tiles, made, tile_loads, tile_stores = refs
        tile = tiles.shape[2]

    def fetch(t):
        copies = []
        first = 0
        for number, part in enumerate(downs):
            rows = part.shape[0]
            src = part.at[:, pl.ds(t * tile, tile)]
            dst = tiles.at[t % 2, pl.ds(first, rows)]
            copies.append(pltpu.make_async_copy(src, dst, tile_loads.at[t % 2, number]))
            first += rows
        return copies

    def store(t):
        dst = y_out[0].at[:, pl.ds(t * tile, tile)]
        return pltpu.make_async_copy(made.at[t % 2], dst, tile_stores.at[t % 2])

    def fill(t):
        if t == 0:
            for copy in fetch(0):
                copy.start()
        if t + 1 < tile_count:
            for copy in fetch(t + 1):
                copy.start()
        for copy in fetch(t):
            copy.wait()
        if t >= 2:
            store(t - 2).wait()
        made[t % 2] = matrix_product(operands[0][...], tiles[t % 2]).astype(made.dtype)
        store(t).start()

    tile_count = y_out[0].shape[1] // tile if downs_n else 0

    folds = []
    settled = {}
    used = {}
    for i, (a, m, n) in enumerate(shapes):
        left, left_first, right, right_first = factors[i]
        factor = (operands[left], left_first, operands[right], right_first)
        for j in list(range(1, a)) + [0]:
            plane = (here + j) % planes_n if a > 1 else 0
            users = used.setdefault((m, n), [])
            depth = slots[m, n].shape[0]
            slot = slots[m, n].at[len(users) % depth]
            piece = Fold(factor, plane, slot, sets[i], j, sends, recvs, len(folds))
            if len(users) >= depth:
                piece.before = users[-depth]
            users.append(piece)
            for plan in plans[i]:
                settled[plan[2]] = len(folds) + 2 * lag
            folds.append((i, j, piece))
    finals = {k: [] for k in range(out_count)}

    def settle(chunk, n):
        i, j, piece = chunk
        place_fold(piece, j, shapes[i], plans[i], outs, own, n, zs, zr, (i, j), finals)

    relays = []
    total = len(folds) + 2 * lag if folds else 0

    def add_relays(source, out, ready, waits):
        nonlocal total
        m, n = source.shape
        for lo in range(0, n, 1536):
            hi = min(n, lo + 1536)

            def block(who, left, right, lo=lo):
                first = pl.multiple_of(who * m, 16)
                return out.at[pl.ds(first, m), pl.ds(lo + left, right - left)]

            number = len(relays)
            part = source.at[:, pl.ds(lo, hi - lo)]
            relay = Relay(part, block, hi - lo, number % 2, relay_sends, relay_recvs, (number,))
            stay = pltpu.make_async_copy(part, block(relay.rank, 0, hi - lo), relay_own.at[number])
            start = max(ready, relays[-1][0] + 1 if relays else 0)
            relays.append((start, relay, stay, waits if lo == 0 else []))
            total = max(total, start + 2 * lag + 1)

    for source, out in zip(sources, wide):
        add_relays(source, out, 0, [])
    for n in sorted(range(len(after)), key=lambda n: settled[after[n]]):
        add_relays(outs[after[n]], later[n], settled[after[n]], finals[after[n]])
    if tiny:
        add_relays(tiny_outs[0], tiny_outs[1], 1, tiny_copies)
    if ring:
        total = max(total, ring.steps)
    if folds:
        folds[0][2].begin()
    for step in range(total):
        if step < len(folds):
            folds[step][2].start()
        if step + 1 < len(folds):
            folds[step + 1][2].begin()
        if 0 <= step - lag < len(folds):
            folds[step - lag][2].middle()
        if 0 <= step - 2 * lag < len(folds):
            folds[step - 2 * lag][2].late()
            settle(folds[step - 2 * lag], step - 2 * lag)
        for start, relay, stay, waits in relays:
            if step == start:
                for copy in waits:
                    copy.wait()
                relay.start()
                stay.start()
            elif step == start + lag:
                relay.middle()
            elif step == start + 2 * lag:
                relay.late()
        if 0 <= step - 1 < tile_count:
            fill(step - 1)
        if ring and step < ring.steps:
            ring.step(step)
    for t in range(max(0, tile_count - 2), tile_count):
        store(t).wait()
    relayed = list(after)
    for out, copies in finals.items():
        if out not in relayed:
            for copy in copies:
                copy.wait()
    for _, relay, stay, _ in relays:
        relay.finish()
        stay.wait()
    for _, _, piece in folds:
        piece.finish()
    if ring:
        ring.finish()


def exchange(
    operands,
    factors,
    shapes,
    plans,
    outs,
    sources,
    after,
    collective_id,
    micros,
    tiny=None,
    ring=(),
    downs=(),
):
    dma = pltpu.SemaphoreType.DMA
    bf16, f32 = jnp.bfloat16, jnp.float32
    any_space = pl.BlockSpec(memory_space=pl.ANY)
    vmem = pl.BlockSpec(memory_space=pltpu.VMEM)
    keys, scratch = fold_scratch(shapes)
    total = max(1, sum(shape[0] for shape in shapes))
    most = 2 * max([len(plan) for plan in plans] + [1])
    deep = max([shape[0] for shape in shapes] + [1])
    widths = [s.shape[1] for s in sources] + [outs[k][1] for k in after]
    relays = 1 + sum(-(-w // 1536) for w in widths)
    wide = [(8 * s.shape[0], s.shape[1]) for s in sources]
    later = [(8 * outs[k][0], outs[k][1]) for k in after]
    shaped = [jax.ShapeDtypeStruct(shape, bf16) for shape in outs + wide + later]
    extras = []
    if tiny is not None:
        planes_n, m, n = tiny.shape
        extras = [tiny]
        shaped += [
            jax.ShapeDtypeStruct((planes_n * m, n), tiny.dtype),
            jax.ShapeDtypeStruct((8 * planes_n * m, n), tiny.dtype),
        ]
    specs = [any_space] * len(shaped)
    scratch += [dma((total, 5))] * 2 + [dma((total, most))]
    scratch += [dma((max(1, len(shapes)), deep, most))] * 2
    scratch += [dma((relays, 8))] * 2 + [dma((relays,))]
    scratch += [dma((4,))] * 2 + [dma((1,))]
    if ring:
        group, tokens, width = ring[0].shape[0], ring[1].shape[0], ring[0].shape[1]
        shaped += [
            jax.ShapeDtypeStruct((group, width), bf16),
            jax.ShapeDtypeStruct((tokens, width), f32),
            jax.ShapeDtypeStruct((1, width), f32),
        ]
        specs += [any_space, vmem, vmem]
        scratch += ring_scratch(group, group // tokens, width, 8)
    if downs:
        hidden = sum(d.shape[0] for d in downs)
        shaped.append(jax.ShapeDtypeStruct((group, width), bf16))
        specs.append(any_space)
        scratch += [
            pltpu.VMEM((2, hidden, 512), bf16),
            pltpu.VMEM((2, group, 512), bf16),
            dma((2, len(downs))),
            dma((2,)),
        ]
    counts = (len(operands), len(ring), len(sources), len(extras), len(outs), list(keys), len(downs))
    results = pl.pallas_call(
        functools.partial(exchange_kernel, (shapes, factors, plans, after, counts)),
        out_shape=shaped,
        in_specs=[vmem] * (len(operands) + len(ring))
        + [any_space] * (len(sources) + len(extras) + len(downs)),
        out_specs=specs,
        scratch_shapes=scratch,
        compiler_params=pltpu.CompilerParams(
            collective_id=collective_id, has_side_effects=True, vmem_limit_bytes=60 * 2**20
        ),
        cost_estimate=pl.CostEstimate(
            flops=0, bytes_accessed=int(micros * 3.0e6), transcendentals=0
        ),
    )(*operands, *ring, *sources, *extras, *downs)
    return results[: len(outs)], results[len(outs) :]


def turn(entries, cosines, sines):
    return entries * cosines + pltpu.roll(entries, HEAD_SIZE // 2, 1) * sines


def readable(begin, first, size, keys):
    place = lax.broadcasted_iota(jnp.int32, (size, keys), 0) + first
    key = lax.broadcasted_iota(jnp.int32, (size, keys), 1)
    return (key >= begin) & (key <= place)


def over_last(left, right):
    return lax.dot_general(
        left, right, (((1,), (1,)), ((), ())), preferred_element_type=jnp.float32
    )


def over_first(left, right):
    return lax.dot_general(
        left, right, (((0,), (0,)), ((), ())), preferred_element_type=jnp.float32
    )


def attend_kernel(x, gain, w, wo, cosines, sines, begin, n1, inverse, q, k, v, o, lse, out):
    f32, bf16 = jnp.float32, jnp.bfloat16
    group, width = x.shape
    heads = q.shape[1] // HEAD_SIZE
    size = 128
    scale = HEAD_SIZE ** (-0.5)

    def norm(step, _):
        at = pl.ds(pl.multiple_of(step * 64, 64), 64)
        rows = x[at, :].astype(f32)
        rms = lax.rsqrt(jnp.mean(rows * rows, axis=-1, keepdims=True) + epsilon)
        inverse[at, :] = jnp.broadcast_to(rms, (64, inverse.shape[1]))
        n1[at, :] = (rows * rms * gain[...]).astype(bf16)
        return 0

    lax.fori_loop(0, group // 64, norm, 0)
    for h in range(heads + 1):
        at = slice(h * HEAD_SIZE, (h + 1) * HEAD_SIZE)
        both = matrix_product(n1[...], w[:, at])
        turned = turn(both, cosines[...], sines[...]).astype(bf16)
        if h < heads:
            q[:, at] = turned
        else:
            k[...] = turned
    v[...] = matrix_product(n1[...], w[:, (heads + 1) * HEAD_SIZE :]).astype(bf16)
    for i in range(group // size):
        rows = slice(i * size, (i + 1) * size)
        keys = (i + 1) * size
        allowed = readable(begin[rows, :], i * size, size, keys)
        lane = lax.broadcasted_iota(jnp.int32, (size, HEAD_SIZE), 1)
        logs = jnp.zeros((size, HEAD_SIZE), f32)
        for h in range(heads):
            at = slice(h * HEAD_SIZE, (h + 1) * HEAD_SIZE)
            scores = over_last(q[rows, at], k[:keys, :]) * scale
            scores = jnp.where(allowed, scores, far_below)
            peak = jnp.max(scores, axis=-1, keepdims=True)
            weights = jnp.exp(scores - peak)
            total = jnp.sum(weights, axis=-1, keepdims=True)
            probs = (weights / total).astype(bf16)
            logs = jnp.where(lane == h, peak + jnp.log(total), logs)
            o[rows, at] = matrix_product(probs, v[:keys, :]).astype(bf16)
        lse[rows, :] = logs

    def project(step, _):
        at = pl.ds(pl.multiple_of(step * 512, 512), 512)
        out[:, at] = matrix_product(o[...], wo[:, at]).astype(bf16)
        return 0

    lax.fori_loop(0, width // 512, project, 0)


def attend(x, gain, w, wo, cosines, sines, begin):
    f32, bf16 = jnp.float32, jnp.bfloat16
    group, width = x.shape
    q_width = w.shape[1] - 2 * HEAD_SIZE
    shaped = [
        ((group, width), bf16),
        ((group, HEAD_SIZE), f32),
        ((group, q_width), bf16),
        ((group, HEAD_SIZE), bf16),
        ((group, HEAD_SIZE), bf16),
        ((group, q_width), bf16),
        ((group, HEAD_SIZE), f32),
        ((group, width), bf16),
    ]
    return pl.pallas_call(
        attend_kernel,
        out_shape=[jax.ShapeDtypeStruct(*s) for s in shaped],
        compiler_params=pltpu.CompilerParams(vmem_limit_bytes=48 * 2**20),
        cost_estimate=pl.CostEstimate(flops=0, bytes_accessed=60000000, transcendentals=0),
    )(x, gain, w, wo, cosines, sines, begin)


def attend_back_kernel(shapes, plans, arrays_n, *refs):
    f32, bf16 = jnp.float32, jnp.bfloat16

    def take(number):
        nonlocal refs
        head, refs = refs[:number], refs[number:]
        return head

    dm, wo, inverse, q, k, v, lse, cosines, sines, begin, o = take(arrays_n)
    tiny_in, source, x_far, w_far, n1_far = take(5)
    dn1, share, wide, tiny_out = take(4)
    dk, dv, dqkv, tiny, tiny_z, x, w, n1, loads = take(9)
    slots, sets = take(2), [take(5), take(5)]
    sends, recvs, own, zs, zr, relay_sends, relay_recvs, relay_own, tiny_s, tiny_r, tiny_own = take(11)
    group, width = dm.shape
    heads = q.shape[1] // HEAD_SIZE
    size = 128
    planes_n = 4
    scale = HEAD_SIZE ** (-0.5)
    rank, core, along_x, along_y, _ = neighbours()
    here = lax.axis_index("shard")
    fetched = []
    for number, (src, dst) in enumerate(((n1_far, n1), (w_far, w), (x_far, x))):
        fetched.append(pltpu.make_async_copy(src, dst, loads.at[number]))
        fetched[-1].start()
    peers = [(along_x, here), (along_y, here), (core, here)]
    greet(peers + [(rank, (here + j) % planes_n) for j in range(1, planes_n)])
    relays, stays = [], []

    def add_relay(part, out, lo):
        m, n = part.shape

        def block(who, left, right):
            first = pl.multiple_of(who * m, 16)
            return out.at[pl.ds(first, m), pl.ds(lo + left, right - left)]

        number = len(relays)
        relays.append(Relay(part, block, n, number % 2, relay_sends, relay_recvs, (number,)))
        stays.append(pltpu.make_async_copy(part, block(rank, 0, n), relay_own.at[number]))
        relays[-1].start()
        stays[-1].start()

    for lo in range(0, source.shape[1], 1536):
        add_relay(source.at[:, pl.ds(lo, 1536)], wide, lo)
    wide_relays = list(relays)
    finals = {0: []}
    outer = Fold((o, 0, dm, 0), 0, slots[1].at[0], sets[1], 0, sends, recvs, 4)
    inner = []
    for n, j in enumerate(list(range(1, planes_n)) + [0]):
        plane = (here + j) % planes_n
        factor = (n1, 0, dqkv, 0)
        inner.append(Fold(factor, plane, slots[0].at[n], sets[0], j, sends, recvs, n))
    outer.begin()
    dk[...] = jnp.zeros_like(dk)
    dv[...] = jnp.zeros_like(dv)
    for h in range(heads):
        at = slice(h * HEAD_SIZE, (h + 1) * HEAD_SIZE)
        upstream = over_last(dm[...], wo[at, :]).astype(bf16)
        for i in range(group // size):
            rows = slice(i * size, (i + 1) * size)
            keys = (i + 1) * size
            allowed = readable(begin[rows, :], i * size, size, keys)
            scores = over_last(q[rows, at], k[:keys, :]) * scale
            probs = jnp.where(allowed, jnp.exp(scores - lse[rows, h : h + 1]), 0.0)
            grad = over_last(upstream[rows, :], v[:keys, :])
            grad = probs * (grad - jnp.sum(probs * grad, axis=-1, keepdims=True))
            grad = grad.astype(bf16)
            dq = matrix_product(grad, k[:keys, :]) * scale
            dqkv[rows, at] = turn(dq, cosines[rows, :], -sines[rows, :]).astype(bf16)
            dk[:keys, :] += over_first(grad, q[rows, at])
            dv[:keys, :] += over_first(probs.astype(bf16), upstream[rows, :])
        if h == 0:
            outer.start()
        if 1 <= h <= len(wide_relays):
            wide_relays[h - 1].middle()
        if 3 <= h:
            wide_relays[h - 3].late()
    at = slice(heads * HEAD_SIZE, (heads + 1) * HEAD_SIZE)
    dqkv[:, at] = turn(dk[...] * scale, cosines[...], -sines[...]).astype(bf16)
    dqkv[:, (heads + 1) * HEAD_SIZE :] = dv[...].astype(bf16)
    rows = w.shape[0] // planes_n
    for plane in range(planes_n):
        tiny[plane] = tiny_in[plane]

    for copy in fetched:
        copy.wait()
    for piece in inner:
        piece.begin()
    for relay in wide_relays[heads - 3 :]:
        relay.late()
    outer.middle()
    for piece in inner:
        piece.start()

    def project(plane, _):
        at = pl.ds(pl.multiple_of(plane * rows, 128), rows)
        grad = over_last(dqkv[...], w[at, :])
        dn1[:, at] = grad.astype(bf16)
        unit = x[:, at].astype(f32) * inverse[:, :1]
        tiny[plane, pl.ds(0, 1), :] = jnp.sum(grad * unit, axis=0, keepdims=True)
        return 0

    lax.fori_loop(0, planes_n, project, 0)
    tiny_copies = []
    m = tiny.shape[1]
    for j in range(planes_n):
        target = (here + j) % planes_n
        dst = tiny_z.at[pl.ds(pl.multiple_of(here * m, 8), m)]
        if j:
            copy = send(tiny.at[target], dst, tiny_s, tiny_r, (j,), (rank, target))
        else:
            copy = pltpu.make_async_copy(tiny.at[here], dst, tiny_own.at[0])
            copy.start()
        tiny_copies.append(copy)
    outer.late()
    place_fold(outer, 0, shapes[1], plans[1], [share], own, 4, zs, zr, (1, 0), finals)
    for n, piece in enumerate(inner):
        piece.middle()
        if n == 1:
            for copy in tiny_copies:
                copy.wait()
            add_relay(tiny_z, tiny_out, 0)
        if n == 3:
            relays[-1].middle()
    for n, piece in enumerate(inner):
        piece.late()
        j = (n + 1) % planes_n
        place_fold(piece, j, shapes[0], plans[0], [share], own, n, zs, zr, (0, j), finals)
    relays[-1].late()
    for copy in finals[0]:
        copy.wait()
    for relay in relays:
        relay.finish()
    for copy in stays:
        copy.wait()
    outer.finish()
    for piece in inner:
        piece.finish()


def attend_back(arrays, later, tiny, source, shapes, plans, share, collective_id):
    f32, bf16 = jnp.float32, jnp.bfloat16
    dm, w = arrays[0], later[1]
    group, width = dm.shape
    planes_n, m, n = tiny.shape
    shaped = [
        ((group, width), bf16),
        (share, bf16),
        ((8 * source.shape[0], source.shape[1]), bf16),
        ((8 * planes_n * m, n), tiny.dtype),
    ]
    relays = source.shape[1] // 1536 + 1
    dma = pltpu.SemaphoreType.DMA
    any_space = pl.BlockSpec(memory_space=pl.ANY)
    vmem = pl.BlockSpec(memory_space=pltpu.VMEM)
    _, buffers = fold_scratch(shapes, 4)
    most = 2 * max(len(plan) for plan in plans)
    return pl.pallas_call(
        functools.partial(attend_back_kernel, shapes, plans, len(arrays)),
        out_shape=[jax.ShapeDtypeStruct(*s) for s in shaped],
        in_specs=[vmem] * (len(arrays) + 1) + [any_space] * 4,
        out_specs=[vmem] + [any_space] * 3,
        scratch_shapes=[pltpu.VMEM((group, HEAD_SIZE), f32)] * 2
        + [
            pltpu.VMEM((group, w.shape[1]), bf16),
            pltpu.VMEM((planes_n, m, n), tiny.dtype),
            pltpu.VMEM((planes_n * m, n), tiny.dtype),
        ]
        + [pltpu.VMEM(a.shape, a.dtype) for a in later]
        + [dma((3,))]
        + buffers
        + [dma((5, 5))] * 2
        + [dma((5, most))]
        + [dma((2, planes_n, most))] * 2
        + [dma((relays, 8))] * 2
        + [dma((relays,))]
        + [dma((planes_n,))] * 2
        + [dma((1,))],
        compiler_params=pltpu.CompilerParams(
            collective_id=collective_id, has_side_effects=True, vmem_limit_bytes=58 * 2**20
        ),
        cost_estimate=pl.CostEstimate(flops=0, bytes_accessed=230000000, transcendentals=0),
    )(*arrays, tiny, source, *later)


def expert_kernel(
    shapes,
    plans,
    n2_far,
    up_far,
    w_up_far,
    w_sd,
    w_e0,
    w_e1,
    router,
    ids,
    inner,
    grad_z,
    dn2,
    grad_router,
    share,
    n2,
    upstream,
    w_up,
    w_down,
    z,
    back,
    routes,
    dlogits,
    loads,
    *refs,
):
    f32, bf16 = jnp.float32, jnp.bfloat16
    slots, refs = refs[:2], refs[2:]
    sets = [refs[5 * n : 5 * n + 5] for n in range(3)]
    sends, recvs, own = refs[15:]
    group, width = n2.shape
    hidden = inner.shape[1]
    sh, ff = hidden // 2, hidden // 4
    tile = 512

    def column(t):
        at = pl.ds(pl.multiple_of(t * tile, 128), tile)
        return pltpu.make_async_copy(w_up_far.at[:, at], w_up.at[:, at], loads.at[t])

    tiles = w_up.shape[1] // tile
    fetched = [pltpu.make_async_copy(n2_far, n2, loads.at[tiles])]
    fetched[0].start()
    for t in range(tiles):
        column(t).start()
    fetched.append(pltpu.make_async_copy(up_far, upstream, loads.at[tiles + 1]))
    first = 0
    for number, part in enumerate((w_sd, w_e0, w_e1)):
        rows = part.shape[0]
        dst = w_down.at[pl.ds(first, rows)]
        fetched.append(pltpu.make_async_copy(part, dst, loads.at[tiles + 2 + number]))
        first += rows
    for copy in fetched[1:]:
        copy.start()
    rank, core, along_x, along_y, _ = neighbours()
    here = lax.axis_index("shard")
    greet([(along_x, here), (along_y, here), (core, here)])
    fetched[0].wait()

    def project(t, _):
        column(t).wait()
        at = pl.ds(pl.multiple_of(t * tile, 128), tile)
        z[:, at] = matrix_product(n2[...], w_up[:, at])
        return 0

    lax.fori_loop(0, tiles, project, 0)
    lane = lax.broadcasted_iota(jnp.int32, (group, 128), 1)
    logits = over_last(n2[...], router[...])
    columns = [logits[:, e : e + 1] for e in range(EXPERTS)]
    peak = functools.reduce(jnp.maximum, columns)
    raised = [jnp.exp(column - peak) for column in columns]
    total = sum(raised)
    table = jnp.zeros((group, 128), f32)
    for e in range(EXPERTS):
        chance = raised[e] / total
        chosen = (ids[...] == e).astype(f32)
        table = jnp.where(lane == e, chance, table)
        table = jnp.where(lane == EXPERTS + e, chosen, table)
    routes[...] = table
    size = 64

    def halves(rows, part):
        if part < 2:
            return z[rows, pl.ds(part * ff, ff)], z[rows, pl.ds(sh + part * ff, ff)]
        left = 2 * sh + (part - 2) * 2 * ff
        return z[rows, pl.ds(left, ff)], z[rows, pl.ds(left + ff, ff)]

    def factor(rows, part):
        e = part - 2
        return routes[rows, e : e + 1] * routes[rows, EXPERTS + e : EXPERTS + e + 1]

    def activate(step, _):
        rows = pl.ds(pl.multiple_of(step * size, size), size)
        for part in range(4):
            gate, up = halves(rows, part)
            value = gate * jax.nn.sigmoid(gate) * up
            if part >= 2:
                value = value * factor(rows, part)
            inner[rows, pl.ds(part * ff, ff)] = value.astype(bf16)
        return 0

    lax.fori_loop(0, group // size, activate, 0)
    for copy in fetched[1:]:
        copy.wait()
    folds = []
    firsts = (0, sh, sh + ff)
    for i in range(3):
        slot = slots[min(i, 1)].at[max(i - 1, 0)]
        folds.append(
            Fold((inner, firsts[i], upstream, 0), 0, slot, sets[i], 0, sends, recvs, i)
        )
    finals = {0: []}
    folds[0].begin()

    def reverse(part):
        back[...] = over_last(upstream[...], w_down[part * ff : (part + 1) * ff, :])

        def rows_back(step, _):
            rows = pl.ds(pl.multiple_of(step * size, size), size)
            gate, up = halves(rows, part)
            grad = back[rows, :]
            sigma = jax.nn.sigmoid(gate)
            active = gate * sigma
            if part >= 2:
                e = part - 2
                weight = jnp.sum(active * up * grad, axis=-1, keepdims=True)
                lanes = lax.broadcasted_iota(jnp.int32, (size, 128), 1)
                routes[rows, :] = jnp.where(lanes == 2 * EXPERTS + e, weight, routes[rows, :])
                grad = grad * factor(rows, part)
                left = 2 * sh + e * 2 * ff
                right = left + ff
            else:
                left, right = part * ff, sh + part * ff
            grad_gate = grad * up * sigma * (1.0 + gate * (1.0 - sigma))
            grad_z[rows, pl.ds(left, ff)] = grad_gate.astype(bf16)
            grad_z[rows, pl.ds(right, ff)] = (grad * active).astype(bf16)
            return 0

        lax.fori_loop(0, group // size, rows_back, 0)

    reverse(0)
    folds[0].start()
    folds[1].begin()
    reverse(1)
    folds[1].start()
    folds[2].begin()
    reverse(2)
    folds[2].start()
    reverse(3)
    folds[0].middle()
    chances = [routes[:, e : e + 1] for e in range(EXPERTS)]
    picked = [routes[:, EXPERTS + e : EXPERTS + e + 1] for e in range(EXPERTS)]
    grads = [
        picked[e] * routes[:, 2 * EXPERTS + e : 2 * EXPERTS + e + 1] for e in range(EXPERTS)
    ]
    mean = sum(chances[e] * grads[e] for e in range(EXPERTS))
    lanes = lax.broadcasted_iota(jnp.int32, (group, dlogits.shape[1]), 1)
    table = jnp.zeros((group, dlogits.shape[1]), f32)
    for e in range(EXPERTS):
        table = jnp.where(lanes == e, chances[e] * (grads[e] - mean), table)
    dlogits[...] = table.astype(bf16)

    def down(t, _):
        at = pl.ds(pl.multiple_of(t * tile, 128), tile)
        grad = over_last(grad_z[...], w_up[at, :])
        grad = grad + matrix_product(dlogits[...], router[:, at])
        dn2[:, at] = grad.astype(bf16)
        return 0

    steps = width // tile
    lax.fori_loop(0, 2, down, 0)
    folds[1].middle()
    lax.fori_loop(2, 4, down, 0)
    folds[2].middle()
    folds[0].late()
    place_fold(folds[0], 0, shapes[0], plans[0], [share], own, 0, None, None, (), finals)
    lax.fori_loop(4, steps, down, 0)
    grad_router[...] = over_first(dlogits[...], n2[...])
    for i in (1, 2):
        folds[i].late()
        place_fold(folds[i], 0, shapes[i], plans[i], [share], own, i, None, None, (), finals)
    for copy in finals[0]:
        copy.wait()
    for piece in folds:
        piece.finish()


def run_experts(n2, upstream, w_up, downs, router, ids, collective_id):
    f32, bf16 = jnp.float32, jnp.bfloat16
    group, width = n2.shape
    hidden = sum(d.shape[0] for d in downs)
    rows = [d.shape[0] // 8 for d in downs]
    shapes = [(1, m, width) for m in rows]
    tops = [sum(rows[:i]) for i in range(3)]
    plans = [[(0, width, 0, 0, top)] for top in tops]
    _, buffers = fold_scratch(shapes)
    shaped = [
        ((group, hidden), bf16),
        ((group, 2 * hidden), bf16),
        ((group, width), bf16),
        ((router.shape[0], width), f32),
        ((sum(rows), width), bf16),
    ]
    dma = pltpu.SemaphoreType.DMA
    any_space = pl.BlockSpec(memory_space=pl.ANY)
    vmem = pl.BlockSpec(memory_space=pltpu.VMEM)
    return pl.pallas_call(
        functools.partial(expert_kernel, shapes, plans),
        out_shape=[jax.ShapeDtypeStruct(*s) for s in shaped],
        in_specs=[any_space] * 6 + [vmem] * 2,
        out_specs=[vmem] * 4 + [any_space],
        scratch_shapes=[
            pltpu.VMEM((group, width), bf16),
            pltpu.VMEM((group, width), bf16),
            pltpu.VMEM(w_up.shape, bf16),
            pltpu.VMEM((hidden, width), bf16),
            pltpu.VMEM((group, 2 * hidden), f32),
            pltpu.VMEM((group, hidden // 4), f32),
            pltpu.VMEM((group, 128), f32),
            pltpu.VMEM((group, router.shape[0]), bf16),
            dma((w_up.shape[1] // 512 + 5,)),
        ]
        + buffers
        + [dma((3, 5))] * 2
        + [dma((3, 2))],
        compiler_params=pltpu.CompilerParams(
            collective_id=collective_id, has_side_effects=True, vmem_limit_bytes=62 * 2**20
        ),
        cost_estimate=pl.CostEstimate(flops=0, bytes_accessed=150000000, transcendentals=0),
    )(n2, upstream, w_up, *downs, router, ids)


def widen_kernel(groups, scattered, order, *refs):
    results = refs[sum(8 if many else 1 for many in scattered) :]

    def write(source, group, at):
        for first, rows, column, size, parts, along_rows in group:
            out = results[at]
            at += 1
            for e in range(parts):
                top = first + (e * rows if along_rows else 0)
                left = column + (0 if along_rows else e * size)
                block = source[pl.ds(top, rows), pl.ds(left, size)].astype(out.dtype)
                if parts == 1:
                    out[...] = block
                else:
                    out[:, e, :] = block

    at = 0
    for group, many in zip(groups, scattered):
        if many:
            for n in range(8):

                @pl.when(order[pl.program_id(0)] == n)
                def _(source=refs[n], group=group, at=at):
                    write(source, group, at)

        else:
            write(refs[0], group, at)
        refs = refs[8 if many else 1 :]
        at += len(group)


def widen(sources, groups, order):
    steps = order.shape[0]
    out_shape, out_specs, in_specs, flat, scattered = [], [], [], [], []
    for group in groups:
        for _, rows, _, size, parts, _ in group:
            if parts == 1:
                out_shape.append(jax.ShapeDtypeStruct((steps * rows, size), jnp.float32))
                out_specs.append(pl.BlockSpec((rows, size), lambda i, order: (i, 0)))
            else:
                out_shape.append(jax.ShapeDtypeStruct((steps * rows, parts, size), jnp.float32))
                out_specs.append(pl.BlockSpec((rows, parts, size), lambda i, order: (i, 0, 0)))
    for s in sources:
        many = isinstance(s, list)
        scattered.append(many)
        for part in s if many else [s]:
            flat.append(part)
            if many:
                in_specs.append(pl.BlockSpec(part.shape, lambda i, order: (0, 0)))
            else:
                block = (part.shape[0] // steps, part.shape[1])
                in_specs.append(pl.BlockSpec(block, lambda i, order: (i, 0)))
    return pl.pallas_call(
        functools.partial(widen_kernel, groups, scattered),
        grid_spec=pltpu.PrefetchScalarGridSpec(
            num_scalar_prefetch=1, grid=(steps,), in_specs=in_specs, out_specs=out_specs
        ),
        out_shape=out_shape,
        compiler_params=pltpu.CompilerParams(vmem_limit_bytes=56 * 2**20),
        cost_estimate=pl.CostEstimate(
            flops=0, bytes_accessed=sum(6 * f.size for f in flat), transcendentals=0
        ),
    )(order, *flat)


def share_out(block, cut, between=None):
    def swap(x, bit):
        return lax.ppermute(x, "replica", [(i, i ^ bit) for i in range(8)])

    along_x, along_y = swap(block, 2), swap(block, 4)
    if between is not None:
        along_x, along_y = between(along_x, along_y)
    far = [swap(x, 1) for x in (block, along_x, along_y)]
    across = jnp.concatenate([swap(along_x[:, :cut], 4), swap(along_y[:, cut:], 2)], axis=1)
    far.append(swap(across, 1))
    return [x for pair in zip((block, along_x, along_y, across), far) for x in pair]


def planes(
    layer_input, cotangent, lengths, expert_ids, g1, wq, wk, wv, wo, g2, wr, w_su, w_sd, w_eu, w_ed
):
    tokens, width = layer_input.shape
    count = lax.axis_size("shard")
    copies = lax.axis_size("replica")
    rows = wq.shape[0]
    piece = rows // copies
    group = tokens * count
    heads = QUERY_HEADS // count
    sh, ff = SH // count, FF // count
    scale = HEAD_SIZE ** (-0.5)
    f32, bf16 = jnp.float32, jnp.bfloat16
    q_width = heads * HEAD_SIZE
    rank = lax.axis_index("replica")
    kv_width = KEY_HEADS * HEAD_SIZE

    def all_tokens(x):
        return lax.all_gather(x, "shard", axis=0, tiled=True)

    def own_tokens(x):
        return lax.psum_scatter(x, "shard", scatter_dimension=0, tiled=True).astype(f32)

    hidden_all = all_tokens(layer_input)
    flags = jnp.pad(expert_ids.reshape(1, tokens).astype(bf16), ((0, 0), (0, rows - tokens)))
    small = jnp.concatenate([g1[None], g2[None], wr.T, flags, jnp.zeros((11, rows), bf16)], axis=0)
    w_qkv, small = spread(
        [wq, wk, wv, small],
        [
            (0, True, 0, q_width, 0, 0),
            (1, True, 0, HEAD_SIZE, 0, q_width),
            (2, True, 0, HEAD_SIZE, 0, q_width + HEAD_SIZE),
        ],
        [(width, q_width + 2 * HEAD_SIZE), (count, 16, rows)],
        True,
        1,
        40,
    )
    gain_one, gain_two = small[:, 0].reshape(width), small[:, 1].reshape(width)
    w_router = small[:, 2 : 2 + EXPERTS].transpose(1, 0, 2).reshape(EXPERTS, width)
    ids = small[:, 2 + EXPERTS, :tokens].reshape(group, 1).astype(jnp.int32)
    cot, w_qkv = lax.optimization_barrier((cotangent, w_qkv))
    upstream = all_tokens(cot)
    w_ed_rows = [w_ed[:, e] for e in range(EXPERTS)]
    mine_eu = lax.dynamic_slice_in_dim(w_eu, rank * piece, piece, axis=0)
    mine_eu = [mine_eu[:, e] for e in range(EXPERTS)]

    _, position = layout(lengths[0], group)
    begin = (jnp.arange(group, dtype=jnp.int32) - position)[:, None]
    cosine_table, sine_table = angles(position)
    cosines = jnp.concatenate([cosine_table, cosine_table], axis=1)
    sines = jnp.concatenate([-sine_table, sine_table], axis=1)
    hidden = layer_input.astype(f32)
    n1, inverse, q, k, v, attended, lse, partial_wo = attend(
        hidden_all, gain_one.astype(f32)[None], w_qkv, wo, cosines, sines, begin
    )
    up_items = [(0, True, 0, sh, 0, 0), (0, True, SH, sh, 0, sh)]
    for e in range(EXPERTS):
        for half in range(2):
            up_items.append((1 + e, False, half * FF, ff, 0, 2 * sh + (2 * e + half) * ff))
    partial_wo, w_su_now = lax.optimization_barrier((partial_wo, w_su))
    w_up, n2, middle, inverse_two = spread(
        [w_su_now, *mine_eu],
        up_items,
        [(width, 2 * sh + 2 * EXPERTS * ff)],
        False,
        2,
        110,
        ring=(partial_wo, layer_input, gain_two.astype(f32)[None]),
    )
    down_parts = [w_sd] + w_ed_rows
    router = jnp.pad(w_router, ((0, 16 - EXPERTS), (0, 0)))
    inner_low, grad_z, grad_n2, grad_router, down_share = run_experts(
        n2, upstream, w_up, down_parts, router, ids, 5
    )
    grad_router = grad_router[:EXPERTS]
    down_rows = [w.shape[0] // copies for w in down_parts]
    plan_su = [(0, sh, 0, 0, 0), (sh, sh, 0, SH, 0)]
    plan_eu = [(n * ff, ff, 1, n * FF, 0) for n in range(2 * EXPERTS)]
    (_, eu_share), (down_all, su_all, grad_proj, grad_middle, grad_gain_two, y) = exchange(
        [inner_low, n2, grad_z],
        [(1, 0, 2, 0), (1, 0, 2, 2 * sh)],
        [(count, piece, 2 * sh), (count, piece, 2 * EXPERTS * ff)],
        [plan_su, plan_eu],
        [(piece, 2 * SH), (piece, 2 * EXPERTS * FF)],
        [down_share],
        [0],
        3,
        150,
        ring=(grad_n2, cotangent, middle, inverse_two, gain_two.astype(f32)[None]),
        downs=down_parts,
    )
    summed = own_tokens(y)
    order = jnp.bitwise_xor(jnp.arange(copies, dtype=jnp.int32), rank)
    tiny = jnp.concatenate(
        [jnp.zeros((1, width), f32), grad_gain_two, grad_router, jnp.zeros((4, width), f32)], axis=0
    )
    tiny = tiny.reshape(8, count, rows).transpose(1, 0, 2)
    plan_qkv = [
        (0, q_width, 0, width, 0),
        (q_width, HEAD_SIZE, 0, 2 * width, 0),
        (q_width + HEAD_SIZE, HEAD_SIZE, 0, 2 * width + kv_width, 0),
    ]
    grad_n1, share, eu_all, tiny = attend_back(
        [grad_proj, wo, inverse, q, k, v, lse, cosines, sines, begin, attended],
        [hidden_all, w_qkv, n1],
        tiny,
        eu_share,
        [(count, piece, q_width + 2 * HEAD_SIZE), (1, piece, width)],
        [plan_qkv, [(0, width, 0, 0, 0)]],
        (piece, 2 * width + 2 * kv_width),
        4,
    )
    grad_n1, summed = lax.optimization_barrier((grad_n1, summed))
    mixed = (middle + summed).astype(bf16)
    grad_n1 = own_tokens(grad_n1)
    share, down_all, su_all = lax.optimization_barrier((share, down_all, su_all))
    mlp_grads = widen(
        [down_all, su_all, eu_all],
        [
            [
                (0, down_rows[0], 0, width, 1, True),
                (down_rows[0], down_rows[1], 0, width, EXPERTS, True),
            ],
            [(0, piece, 0, 2 * SH, 1, True)],
            [(0, piece, 0, 2 * FF, EXPERTS, False)],
        ],
        order,
    )

    def beside(*blocks):
        nonlocal mlp_grads
        *blocks, mlp_grads = lax.optimization_barrier((*blocks, mlp_grads))
        return blocks

    att_all = share_out(share, EXPERTS * FF, beside)
    sd_grad, ed_grad, su_grad, eu_grad = mlp_grads
    wo_grad, wq_grad, wk_grad, wv_grad = widen(
        [att_all],
        [
            [
                (0, piece, 0, width, 1, True),
                (0, piece, width, width, 1, True),
                (0, piece, 2 * width, kv_width, 1, True),
                (0, piece, 2 * width + kv_width, kv_width, 1, True),
            ],
        ],
        order,
    )
    tiny = jnp.sum(tiny.reshape(copies * count, 8, rows), axis=0)
    unit_one, rms_one = norm_forward(hidden)
    grad_hidden, _ = norm_backward(grad_n1, unit_one, rms_one, gain_one)
    input_grad = (grad_middle + grad_hidden).astype(bf16)

    return (
        mixed,
        input_grad,
        tiny[0],
        wq_grad,
        wk_grad,
        wv_grad,
        wo_grad,
        tiny[1],
        tiny[2 : 2 + EXPERTS].T,
        su_grad,
        sd_grad,
        eu_grad,
        ed_grad,
    )


def solution(mesh):
    return jax.shard_map(
        planes if mesh.shape["shard"] == KEY_HEADS and mesh.shape["replica"] == 8 else shards,
        mesh=mesh,
        in_specs=(
            P(("replica", "shard"), None),
            P(("replica", "shard"), None),
            P("replica", None),
            P(("replica", "shard"), None),
            P("shard"),
            P("shard", None),
            P("shard", None),
            P("shard", None),
            P("shard", None),
            P("shard"),
            P("shard", None),
            P("shard", None),
            P("shard", None),
            P("shard", None, None),
            P("shard", None, None),
        ),
        out_specs=(
            P(("replica", "shard"), None),
            P(("replica", "shard"), None),
            P("shard"),
            P("shard", None),
            P("shard", None),
            P("shard", None),
            P("shard", None),
            P("shard"),
            P("shard", None),
            P("shard", None),
            P("shard", None),
            P("shard", None, None),
            P("shard", None, None),
        ),
        check_vma=False,
    )
```
